32 devices in a mesh: groups: 2 (over x), wide: 8 (over z, y), narrow: 2 (over core).
Axes of the slice: x: 2, y: 2, z: 4, core: 2. Of those that a mesh axis runs over, the one named last changes fastest.
Arguments:
- tokens: bfloat16 [4096, 4096], P(('groups', 'wide')), parts along dimension 0, may hold values from -6 to 6
- norm_gain: float32 [4096], replicated, may hold values from 0.1 to 1.9
- w_in: bfloat16 [4096, 1024], P('wide'), may hold values from -0.09375 to 0.09375
- w_out: bfloat16 [1024, 4096], P('wide', 'narrow'), may hold values from -0.1875 to 0.1875
- w_up: bfloat16 [8, 1024, 2688], P('wide', None, 'narrow'), may hold values from -0.1875 to 0.1875
- w_down: bfloat16 [8, 2688, 1024], P('wide', 'narrow'), may hold values from -0.15625 to 0.15625
- expert_ids: int32 [4096, 4], P(('groups', 'wide')), parts along dimension 0, may hold values from 0 to 7, all different within a row; in each aligned block of 256 rows (0 to 255, 256 to 511, ...) at most 192 rows name the same one
- gate_weights: float32 [4096, 4], P(('groups', 'wide')), parts along dimension 0, may hold values from 0.1 to 1
Outputs:
- result: bfloat16 [4096, 4096], P(('groups', 'wide'), 'narrow'), parts along dimension 0
The draws below stay inside these ranges and needn't reach their ends.
There are 2 independent parts, one for each index of `groups`. The reference program is written for one: setup_inputs(seed, part) draws one part's arguments, and reference() takes and returns one part's arrays. A program takes and returns all parts, laid end to end along the dimension named above; an argument that names none is the same for every part. Nothing has to cross between parts.
Inputs may be any that keep to these rules, and one draw needn't show every extreme that they name: `expert_ids`: within the 256 rows of one index of wide, the entries of a row differ and no expert is named by more than 192 rows.
All inputs are finite; a program needn't handle non-finite values.
Results may differ from the reference program's by a relative error of at most 0.013.
Values may be sent and summed in bfloat16 or wider, within the bound.
No kernel may reach another device: no remote copies, remote signals or barrier semaphores. Data moves between devices by JAX's collectives and lax.ppermute only.
A program may use at most 128 MiB of HBM per device.

```python
import math
import jax
import jax.numpy as jnp
import numpy as np
from jax import lax

D = 4096
L = 1024
HID = 2688
TOPK = 4
TOK_DEV = 256
EXPERTS = 8
CAP = 192
TOKENS = 2048


def level_of(rng, dims, cuts, low, largest):
    def one(axis_at, parts):
        steps = jax.random.uniform(jax.random.fold_in(jax.random.fold_in(rng, 6), axis_at), (parts,), jnp.float32, low / len(cuts), largest / len(cuts))
        return jnp.repeat(jnp.exp(steps), dims[axis_at] // parts).reshape((-1,) + (1,) * (len(dims) - axis_at - 1))

    gain = one(*cuts[0])
    for cut in cuts[1:]:
        gain = gain * one(*cut)
    return gain


def deal_out(own_key, own, number, rows, number_of, top, limit, slope):
    order = jax.random.permutation(own_key, number_of)
    crowded, ordinary = load_shares(number_of, rows * top, limit, slope, True), load_shares(number_of, rows * top, limit, slope, False)
    places = jnp.arange(number_of)

    def named(sizes, rotation):
        used = int((sizes > 0).sum())
        fixed = max(1, used // 4)
        moved = fixed + (places - fixed + rotation * (used - fixed)) % max(1, number_of - fixed)
        return jnp.zeros((number_of,), jnp.int32).at[order[jnp.where(places < fixed, places, moved)]].set(jnp.asarray(sizes, jnp.int32))

    sizes = jnp.where(number % 4 == 0, named(crowded, number // 4), named(ordinary, number - number // 4 - 1))
    mixed = jax.random.permutation(jax.random.fold_in(own, 3), number_of)
    donor, taker = mixed[0:number_of // 2 * 2:2], mixed[1:number_of // 2 * 2:2]
    slack = jnp.minimum(sizes[donor] - 1, limit - sizes[taker]) // 2
    slack = jnp.where((donor == order[0]) | (taker == order[0]) | (sizes[taker] == 0), 0, jnp.maximum(slack, 0))
    moved = jax.random.randint(jax.random.fold_in(own, 4), (number_of // 2,), 0, 1 << 20) % (slack + 1)
    sizes = sizes.at[donor].add(-moved).at[taker].add(moved)
    items = jnp.searchsorted(jnp.cumsum(sizes), jnp.arange(rows * top), side="right").astype(jnp.int32)
    grid = items.reshape(top, rows).T
    grid = grid[jax.random.permutation(jax.random.fold_in(own, 1), rows)]
    rotation = jax.random.randint(jax.random.fold_in(own, 2), (rows, 1), 0, top)
    return jnp.take_along_axis(grid, (jnp.arange(top)[None, :] + rotation) % top, axis=1)


def load_shares(amount, total, limit, lean, full):
    weights = [(1 << 20) // math.isqrt(grade ** lean) + 1 for grade in range(1, amount + 1)]
    largest = limit if full else min(limit, max(-(-total // amount), total * weights[0] // sum(weights)))
    least = 1 if total - largest >= amount - 1 else 0
    given, spare = [largest] + [least] * (amount - 1), total - largest - least * (amount - 1)
    while spare > 0:
        candidates = [i for i in range(1, amount) if given[i] < largest] or [i for i in range(1, amount) if given[i] < limit]
        mass, budget = sum([weights[i] for i in candidates]), spare
        for i in candidates:
            more = min(limit - given[i], max(1, budget * weights[i] // mass), spare)
            given[i] = given[i] + more
            spare = spare - more
    return np.array(given)


def noise(key, shape, deviation, reach, split=(), kind=jnp.bfloat16):
    result = deviation * jax.random.normal(key, shape, jnp.float32)
    if split:
        result = result * level_of(key, shape, split, -0.22, 0.18)
    return jnp.clip(result, -reach, reach).astype(kind)


def setup_inputs(seed: int = 0, part: int = 0) -> dict:
    seeds = jax.random.split(jax.random.key(seed), 9)
    own_keys = jax.random.split(jax.random.fold_in(seeds[8], part), 9)
    tokens = noise(own_keys[0], (TOKENS, D), 1.0, 6.0, ((0, 8),))
    norm_gain = jnp.clip(1.0 + 0.18 * jax.random.normal(seeds[1], (D,), jnp.float32), 0.1, 1.9)
    w_in = noise(seeds[2], (D, L), D ** -0.5, 0.09375, ((0, 8),))
    w_out = noise(seeds[3], (L, D), L ** -0.5, 0.1875, ((0, 8), (1, 2)))
    w_up = noise(seeds[4], (EXPERTS, L, HID), L ** -0.5, 0.1875, ((0, 8), (2, 2)))
    w_down = noise(seeds[5], (EXPERTS, HID, L), (HID // 2) ** -0.5, 0.15625, ((0, 8), (1, 2)))
    expert_ids_keys = jax.random.split(jax.random.fold_in(own_keys[6], 1), TOKENS // TOK_DEV)
    expert_ids_turns = jax.random.permutation(jax.random.fold_in(own_keys[6], 3), TOKENS // TOK_DEV)
    expert_ids = jax.vmap(lambda own, number: deal_out(jax.random.fold_in(own_keys[6], 2), own, number, TOK_DEV, EXPERTS, TOPK, CAP, 1))(expert_ids_keys, expert_ids_turns).reshape((TOKENS, TOPK))
    gate_weights = jnp.clip(jnp.exp(math.log(1.0) - 2.3025851 * jax.random.uniform(own_keys[7], (TOKENS, TOPK), jnp.float32) ** level_of(own_keys[7], (TOKENS, TOPK), ((0, 8),), -0.2, 0.2)), 0.1, 1.0)
    return {"tokens": tokens, "norm_gain": norm_gain, "w_in": w_in, "w_out": w_out, "w_up": w_up, "w_down": w_down, "expert_ids": expert_ids, "gate_weights": gate_weights}


def reference(tokens, norm_gain, w_in, w_out, w_up, w_down, expert_ids, gate_weights):
    widened = tokens.astype(jnp.float32)
    scale = lax.rsqrt(lax.optimization_barrier(jnp.mean(widened * widened, axis=-1, keepdims=True)) + 1e-05)
    normed = (widened * scale * norm_gain).astype(jnp.bfloat16)
    latent = jnp.dot(normed, w_in, preferred_element_type=jnp.float32).astype(jnp.bfloat16)
    blocks = TOKENS // TOK_DEV
    per_block = expert_ids.reshape(blocks, TOK_DEV * TOPK)
    onehot = (per_block[:, :, None] == jnp.arange(EXPERTS, dtype=jnp.int32)[None, None, :]).astype(jnp.int32)
    slot_index = lax.optimization_barrier(jnp.sum((jnp.cumsum(onehot, axis=1) - 1) * onehot, axis=-1))
    block_index = jnp.arange(blocks, dtype=jnp.int32)[:, None]
    rows_expert = blocks * CAP
    target = (per_block * rows_expert + block_index * CAP + slot_index).reshape(-1).astype(jnp.int32)
    repeated = jnp.repeat(latent, TOPK, axis=0)
    inputs = jnp.zeros((EXPERTS * rows_expert, L), jnp.bfloat16).at[target].set(repeated)
    inputs = inputs.reshape(EXPERTS, rows_expert, L)

    def one_expert(packed):
        rows, up_weight, down_weight = packed
        hidden = jnp.dot(rows, up_weight, preferred_element_type=jnp.float32)
        hidden = jnp.square(jnp.maximum(hidden, 0.0)).astype(jnp.bfloat16)
        return jnp.dot(hidden, down_weight, preferred_element_type=jnp.float32).astype(jnp.bfloat16)
    outputs = lax.map(one_expert, (inputs, w_up, w_down)).reshape(EXPERTS * rows_expert, L)
    picked = outputs[target].astype(jnp.float32).reshape(TOKENS, TOPK, L)
    mixture = lax.optimization_barrier(jnp.sum(picked * gate_weights[:, :, None], axis=1)).astype(jnp.bfloat16)
    branch = jnp.dot(mixture, w_out, preferred_element_type=jnp.float32)
    return (widened + branch).astype(jnp.bfloat16)
```

```python
import jax
import jax.numpy as jnp
from jax import lax
from jax.sharding import PartitionSpec as P


def ring_order(mesh):
    wide = mesh.shape["wide"]
    line = mesh.devices.reshape(-1, wide, mesh.shape["narrow"])[0, :, 0]
    places = [tuple(getattr(d, "coords", (0,))) for d in line]
    spread = [len(set(c)) for c in zip(*places)]
    if sum(s > 1 for s in spread) == 2 and wide % 2 == 0:
        return list(range(0, wide, 2)) + list(range(wide - 1, 0, -2))
    return list(range(wide))


def make_local(order):
    wide = len(order)
    far = wide // 2
    up_perm = [(order[i], order[(i + 1) % wide]) for i in range(wide)]
    down_perm = [(order[(i + 1) % wide], order[i]) for i in range(wide)]
    place_of = [order.index(i) for i in range(wide)]

    def local(tokens, norm_gain, w_in, w_out, w_up, w_down, expert_ids, gate_weights):
        f32, bf16 = jnp.float32, jnp.bfloat16
        groups = lax.axis_size("groups")
        side = lax.axis_index("groups") % 2
        me = lax.axis_index("wide")
        core = lax.axis_index("narrow")
        rows, model = tokens.shape
        half_rows = rows // 2
        width = w_in.shape[1]
        half, quarter = width // 2, width // 4
        depth = w_in.shape[0]
        place = jnp.asarray(place_of)[me]

        def up(x):
            return lax.ppermute(x, "wide", up_perm)

        def down(x):
            return lax.ppermute(x, "wide", down_perm)

        def swap(x):
            return lax.ppermute(x, "narrow", [(0, 1), (1, 0)])

        def across(x):
            return lax.ppermute(x, "groups", [(i, i ^ 1) for i in range(groups)])

        def at(distance):
            return jnp.asarray(order)[(place + distance) % wide]

        def ordered(first, mine, other, axis):
            return jnp.concatenate(
                [jnp.where(first, mine, other), jnp.where(first, other, mine)], axis
            )

        named = expert_ids[:, :, None] == jnp.arange(wide, dtype=jnp.int32)
        dense = jnp.sum(jnp.where(named, gate_weights[:, :, None], 0.0), axis=1).T
        gates = lax.all_gather(dense, "wide", axis=0)
        gates = lax.dynamic_index_in_dim(gates, me, 1, keepdims=False)

        full_out = lax.all_gather(w_out, "wide", axis=0, tiled=True)

        own = lax.dynamic_slice_in_dim(w_in, (core * 2 + side) * quarter, quarter, 1)
        full_in = jnp.zeros((depth * wide, quarter), bf16)
        full_in = lax.dynamic_update_slice_in_dim(full_in, own, me * depth, 0)
        from_below = from_above = own
        for d in range(1, far + 1):
            if d == far:
                cut = depth // 2
                from_below = up(from_below[:cut])
                from_above = down(from_above[cut:])
                begin = at(far) * depth
                full_in = lax.dynamic_update_slice_in_dim(full_in, from_below, begin, 0)
                full_in = lax.dynamic_update_slice_in_dim(
                    full_in, from_above, begin + cut, 0
                )
            else:
                from_below, from_above = up(from_below), down(from_above)
                full_in = lax.dynamic_update_slice_in_dim(
                    full_in, from_below, at(-d) * depth, 0
                )
                full_in = lax.dynamic_update_slice_in_dim(
                    full_in, from_above, at(d) * depth, 0
                )

        widened = tokens.astype(f32)
        scale = lax.rsqrt(jnp.mean(widened * widened, axis=-1, keepdims=True) + 1e-05)
        normed = (widened * scale * norm_gain).astype(bf16)
        there = across(lax.dynamic_slice_in_dim(normed, core * half_rows, half_rows, 0))
        there = jnp.concatenate([there, swap(there)], axis=0)
        lat_there = jnp.dot(there, full_in, preferred_element_type=f32).astype(bf16)
        lat_other = across(lat_there)
        lat_mine = jnp.dot(normed, full_in, preferred_element_type=f32).astype(bf16)
        lat_other = ordered(core == 0, lat_other[:half_rows], lat_other[half_rows:], 0)
        latent = ordered(side == 0, lat_mine, lat_other, 1)

        up_weight = w_up[0]
        up_weight = jnp.concatenate(
            [
                lax.dynamic_slice_in_dim(up_weight, core * half, half, 0),
                lax.dynamic_slice_in_dim(up_weight, (1 - core) * half, half, 0),
            ],
            axis=0,
        )
        down_weight = w_down[0]
        down_weight = jnp.concatenate(
            [
                lax.dynamic_slice_in_dim(down_weight, core * half, half, 1),
                lax.dynamic_slice_in_dim(down_weight, (1 - core) * half, half, 1),
            ],
            axis=1,
        )

        def expert(x, gate):
            x = jnp.concatenate([x, swap(x)], axis=1)
            hidden = jnp.dot(x, up_weight, preferred_element_type=f32)
            hidden = jnp.square(jnp.maximum(hidden, 0.0)).astype(bf16)
            part = jnp.dot(hidden, down_weight, preferred_element_type=f32)
            part = (part * gate[:, None]).astype(bf16)
            return part[:, :half].astype(f32) + swap(part[:, half:]).astype(f32)

        def gate_of(distance):
            return lax.dynamic_index_in_dim(gates, at(distance), 0, keepdims=False)

        from_below = from_above = latent
        arrived = [(latent, gate_of(0))]
        for d in range(1, far + 1):
            if d == far:
                from_below = up(from_below[:half_rows])
                from_above = down(from_above[half_rows:])
                gate = gate_of(far)
            else:
                from_below, from_above = up(from_below), down(from_above)
                gate = jnp.concatenate([gate_of(-d), gate_of(d)])
            arrived.append((jnp.concatenate([from_below, from_above], axis=0), gate))
        parts = [expert(x, gate) for x, gate in arrived]

        to_above = up(parts[far][:half_rows].astype(bf16)).astype(f32)
        to_below = down(parts[far][half_rows:].astype(bf16)).astype(f32)
        for d in range(far - 1, 0, -1):
            below, above = parts[d][:rows], parts[d][rows:]
            if d == far - 1:
                above = jnp.concatenate(
                    [above[:half_rows] + to_above, above[half_rows:]], axis=0
                )
                below = jnp.concatenate(
                    [below[:half_rows], below[half_rows:] + to_below], axis=0
                )
            else:
                above, below = above + to_above, below + to_below
            to_above = up(above.astype(bf16)).astype(f32)
            to_below = down(below.astype(bf16)).astype(f32)
        mixture = (parts[0] + to_above + to_below).astype(bf16)
        mixture = ordered(core == 0, mixture, swap(mixture), 1)

        branch = jnp.dot(mixture, full_out, preferred_element_type=f32)
        columns = full_out.shape[1]
        kept = lax.dynamic_slice_in_dim(tokens, core * columns, columns, 1)
        return (kept.astype(f32) + branch).astype(bf16)

    return local


def solution(mesh):
    in_specs = (
        P(("groups", "wide"), None),
        P(),
        P("wide", None),
        P("wide", "narrow"),
        P("wide", None, "narrow"),
        P("wide", "narrow", None),
        P(("groups", "wide"), None),
        P(("groups", "wide"), None),
    )
    out_specs = P(("groups", "wide"), "narrow")
    local = make_local(ring_order(mesh))
    return jax.shard_map(
        local, mesh=mesh, in_specs=in_specs, out_specs=out_specs, check_vma=False
    )
```

```python
import functools

import jax
import jax.numpy as jnp
from jax import lax
from jax.experimental import pallas as pl
from jax.experimental.pallas import tpu as pltpu
from jax.sharding import PartitionSpec as P

F32, BF16 = jnp.float32, jnp.bfloat16
VMEM = pl.BlockSpec(memory_space=pltpu.VMEM)
SMEM = pl.BlockSpec(memory_space=pltpu.SMEM)
ANY = pl.BlockSpec(memory_space=pl.ANY)
LIMIT, BIG = 40 * 2**20, 60 * 2**20


def kernel_call(body, out, n_in, flops, nbytes, scratch=(), n_any=0, limit=LIMIT):
    return pl.pallas_call(
        body,
        out_shape=out,
        in_specs=[SMEM] + [VMEM] * (n_in - 1) + [ANY] * n_any,
        out_specs=jax.tree.map(lambda _: VMEM, out),
        scratch_shapes=list(scratch),
        compiler_params=pltpu.CompilerParams(vmem_limit_bytes=limit),
        cost_estimate=pl.CostEstimate(
            flops=flops, bytes_accessed=nbytes, transcendentals=0
        ),
    )


def norm_body(info, tokens, gain, out):
    rows, model = tokens.shape
    step = 16

    @pl.loop(0, rows // step)
    def _(i):
        at = pl.ds(pl.multiple_of(i * step, step), step)
        x = tokens[at, :].astype(F32)
        mean = jnp.sum(x * x, axis=1, keepdims=True) * (1.0 / model)
        x = tokens[at, :].astype(F32) * lax.rsqrt(mean + 1e-05) * gain[...]
        out[at, :] = x.astype(BF16)


def fetch(sources, places, done):
    copies = [
        pltpu.make_async_copy(a, b, done.at[i])
        for i, (a, b) in enumerate(zip(sources, places))
    ]
    for copy in copies:
        copy.start()

    def arrived(i):
        copies[i].wait()
        return places[i]

    return arrived


def places_for(arrays):
    return [pltpu.VMEM(a.shape, a.dtype) for a in arrays] + [
        pltpu.SemaphoreType.DMA((len(arrays),))
    ]


def project(info, left, count, depth, arrived):
    total = None
    for i in range(count - 1):
        if i < count - 2:
            block = arrived(i)[:depth, :]
        else:
            block = [arrived(j)[: depth // 2, :] for j in (i, i + 1)]
            block = jnp.concatenate(block, axis=0)
        begin = pl.multiple_of(info[2 + i] * depth, depth)
        term = jnp.dot(left(pl.ds(begin, depth)), block, preferred_element_type=F32)
        total = term if total is None else total + term
    return total


def there_body(depth, info, first, second, *rest):
    count = len(rest) // 2 - 1
    blocks, out, places, done = rest[:count], rest[count], rest[count + 1 : -1], rest[-1]
    half = first.shape[0]
    total = project(
        info,
        lambda at: jnp.concatenate([first[:, at], second[:, at]], axis=0),
        count,
        depth,
        fetch(blocks, places, done),
    ).astype(BF16)
    core = info[0]
    out[pl.ds(pl.multiple_of(core * half, half), half), :] = total[:half]
    out[pl.ds(pl.multiple_of((1 - core) * half, half), half), :] = total[half:]


def mine_body(depth, wide, info, normed, *rest):
    count = (len(rest) - 3) // 2
    blocks, out, gates = rest[:count], rest[count], rest[count + 1]
    places, done = rest[count + 2 : -1], rest[-1]
    total = project(
        info, lambda at: normed[:, at], count, depth, fetch(blocks, places, done)
    )
    out[...] = total.astype(BF16)
    blocks = places
    carried = [b[depth:, :] for b in blocks[:-2]] + [blocks[-1][depth // 2 :, :]]
    number = lax.broadcasted_iota(jnp.int32, carried[0].shape, 0)
    chosen = (number % wide == info[1]) & (number < 3 * wide)
    lines = [
        jnp.sum(jnp.where(chosen, c.astype(F32), 0.0), axis=0, keepdims=True)
        for c in carried
    ]
    gates[...] = jnp.concatenate(lines, axis=0).T


def expert_body(columns, info, *refs):
    n = len(columns)
    own, other = refs[:n], refs[n : 2 * n]
    gates, up, down, stay, give, x, total = refs[2 * n :]
    core = info[0]
    half = own[0].shape[1]
    here = pl.ds(pl.multiple_of(core * half, half), half)
    there = pl.ds(pl.multiple_of((1 - core) * half, half), half)
    begin = 0
    for a, b in zip(own, other):
        size = a.shape[0]
        x[begin : begin + size, here] = a[...]
        x[begin : begin + size, there] = b[...]
        begin += size
    hidden = up.shape[0]
    chunk = max(c for c in range(16, 513, 16) if hidden % c == 0)
    for i in range(hidden // chunk):
        at = slice(i * chunk, (i + 1) * chunk)
        h = lax.dot_general(
            x[...], up[at, :], (((1,), (1,)), ((), ())), preferred_element_type=F32
        )
        h = jnp.square(jnp.maximum(h, 0.0)).astype(BF16)
        part = jnp.dot(h, down[at, :], preferred_element_type=F32)
        if i == 0:
            total[...] = part
        else:
            total[...] += part
    begin = 0
    for j, (column, first) in enumerate(columns):
        size = own[j].shape[0]
        gate = gates[first : first + size, column : column + 1]
        rows = slice(begin, begin + size)
        stay[rows, :] = (total[rows, here] * gate).astype(BF16)
        give[rows, :] = (total[rows, there] * gate).astype(BF16)
        begin += size


def final_body(depth, info, kept, mine, back, *rest):
    *blocks, out, mixture, full, done = rest
    core, side, me = info[0], info[1], info[2]
    count = (len(blocks) - 1) // 2
    span = blocks[1].shape[1]
    places = [full.at[pl.ds(pl.multiple_of(me * depth, depth), depth), :]]
    for number in range(2):
        at = pl.ds(pl.multiple_of((side + number) % 2 * span, span), span)
        for i in range(count):
            size = blocks[1 + i].shape[0]
            begin = info[2 + min(1 + i, count - 1)] * depth
            if i == count - 1:
                begin = begin + size
            places.append(full.at[pl.ds(pl.multiple_of(begin, size), size), at])
    arrived = fetch(blocks, places, done)
    half = mine.shape[1]
    mixture[:, pl.ds(pl.multiple_of(core * half, half), half)] = mine[...]
    mixture[:, pl.ds(pl.multiple_of((1 - core) * half, half), half)] = back[...]
    for i in range(len(blocks)):
        arrived(i)
    step = 512
    for i in range(full.shape[1] // step):
        at = slice(i * step, (i + 1) * step)
        branch = jnp.dot(mixture[...], full[:, at], preferred_element_type=F32)
        out[:, at] = (kept[:, at].astype(F32) + branch).astype(BF16)


def after(x, *others):
    return lax.optimization_barrier((x, others))[0]


def both(*xs):
    return lax.optimization_barrier(xs)


def ring_order(mesh):
    wide = mesh.shape["wide"]
    line = mesh.devices.reshape(-1, wide, mesh.shape["narrow"])[0, :, 0]
    places = [tuple(getattr(d, "coords", (0,))) for d in line]
    spread = [len(set(c)) for c in zip(*places)]
    if sum(s > 1 for s in spread) == 2 and wide % 2 == 0:
        return list(range(0, wide, 2)) + list(range(wide - 1, 0, -2))
    return list(range(wide))


def make_local(order):
    wide = len(order)
    far = wide // 2
    up_perm = [(order[i], order[(i + 1) % wide]) for i in range(wide)]
    down_perm = [(order[(i + 1) % wide], order[i]) for i in range(wide)]
    offsets = [0] + [s * d for d in range(1, far) for s in (-1, 1)] + [far]
    sources = [[order[(order.index(i) + o) % wide] for o in offsets] for i in range(wide)]

    def local(tokens, norm_gain, w_in, w_out, w_up, w_down, expert_ids, gate_weights):
        groups = lax.axis_size("groups")
        side = lax.axis_index("groups") % 2
        me = lax.axis_index("wide")
        core = lax.axis_index("narrow")
        rows, model = tokens.shape
        half_rows = rows // 2
        depth, width = w_in.shape
        half, quarter = width // 2, width // 4
        info = jnp.concatenate(
            [jnp.stack([core, me]), jnp.asarray(sources, jnp.int32)[me]]
        ).astype(jnp.int32)

        def up(x):
            return lax.ppermute(x, "wide", up_perm)

        def down(x):
            return lax.ppermute(x, "wide", down_perm)

        def swap(x):
            return lax.ppermute(x, "narrow", [(0, 1), (1, 0)])

        def across(x):
            return lax.ppermute(x, "groups", [(i, i ^ 1) for i in range(groups)])

        def shape(*dims, kind=BF16):
            return jax.ShapeDtypeStruct(dims, kind)

        named = expert_ids[:, :, None] == jnp.arange(wide, dtype=jnp.int32)
        dense = jnp.sum(jnp.where(named, gate_weights[:, :, None], 0.0), axis=1).T
        high = dense.astype(BF16)
        rest = dense - high.astype(F32)
        middle = rest.astype(BF16)
        low = (rest - middle.astype(F32)).astype(BF16)
        empty = jnp.zeros((-3 * wide % 16, rows), BF16)

        block = lax.dynamic_slice_in_dim(w_in, (core * 2 + side) * quarter, quarter, 1)
        block = jnp.concatenate([block, high, middle, low, empty], axis=0)
        blocks = [block]
        below = above = block
        for _ in range(1, far):
            below, above = both(up(below), down(above))
            blocks += [below, above]
        blocks += both(up(below[: depth // 2]), down(above[depth // 2 :]))

        def norm(x):
            return kernel_call(
                norm_body,
                shape(*x.shape),
                3,
                8 * x.size,
                4 * x.size,
            )(info, x, norm_gain.reshape(1, model))

        normed = norm(after(tokens, block))
        raw = lax.dynamic_slice_in_dim(after(tokens, block), core * half_rows, half_rows, 0)
        first = norm(after(across(raw), blocks[-3], normed))
        second = swap(first)
        columns = w_out.shape[1]
        kept = lax.dynamic_slice_in_dim(tokens, core * columns, columns, 1)

        out_depth = w_out.shape[0]
        out_blocks = []
        out_below = out_above = lax.dynamic_slice_in_dim(
            w_out, side * (columns // 2), columns // 2, 1
        )

        def out_step(*others):
            nonlocal out_below, out_above
            out_below, out_above = after((out_below, out_above), *others)
            if len(out_blocks) == 2 * far - 2:
                cut = out_depth // 2
                out_below, out_above = out_below[:cut], out_above[cut:]
            out_below, out_above = both(up(out_below), down(out_above))
            out_blocks.extend([out_below, out_above])

        early = far // 2
        out_step(blocks[-3], blocks[-4])
        for _ in range(1, early):
            out_step()

        flops = 2 * rows * model * quarter
        nbytes = 2 * (rows * model + model * quarter)
        lat_there = kernel_call(
            functools.partial(there_body, depth),
            shape(rows, quarter),
            3,
            flops,
            nbytes,
            places_for(blocks),
            len(blocks),
            BIG,
        )(info, first, second, *blocks)
        lat_other = across(lat_there)
        lat_mine, gates = kernel_call(
            functools.partial(mine_body, depth, wide),
            (shape(rows, quarter), shape(rows, wide, kind=F32)),
            2,
            flops,
            nbytes,
            places_for(blocks),
            len(blocks),
            BIG,
        )(info, after(normed, lat_there), *blocks)
        latent = jnp.concatenate(
            [
                jnp.where(side == 0, lat_mine, lat_other),
                jnp.where(side == 0, lat_other, lat_mine),
            ],
            axis=1,
        )
        latent = after(latent, *out_blocks[:-2])

        up_weight, down_weight = w_up[0].T, w_down[0]
        hidden = up_weight.shape[0]

        def expert(xs, columns, *others):
            size = sum(x.shape[0] for x in xs)
            out = shape(size, half)
            ys = after([swap(x) for x in xs], *others)
            return kernel_call(
                functools.partial(expert_body, columns),
                (out, out),
                4 + 2 * len(xs),
                4 * size * width * hidden,
                4 * hidden * width + 4 * size * width,
                [pltpu.VMEM((size, width), BF16), pltpu.VMEM((size, width), F32)],
            )(info, *xs, *ys, gates, up_weight, down_weight)

        def total(stay, given, more=None):
            t = stay.astype(F32) + given.astype(F32)
            return t if more is None else t + more.astype(F32)

        def hand(first, number):
            handed.extend(both(*[across(b) for b in out_blocks[first : first + number]]))

        handed = []
        done = {0: expert([latent], [(0, 0)])}
        pairs = [(latent, latent)]
        for d in range(1, far + 1):
            below, above = pairs[-1]
            if d == 2:
                below, above = after((below, above), *done[0], *out_blocks)
            if d == 3:
                hand(0, 2)
                below, above = after((below, above), *handed)
            if d == far:
                below, above = after((below, above), *done[1])
                below, above = below[:half_rows], above[half_rows:]
            pairs.append(both(up(below), down(above)))
            if d == 2:
                done[1] = expert(pairs[1], [(1, 0), (2, 0)])
        hand(len(handed), 2)
        out_step(*pairs[far - 1])
        done[far] = expert(pairs[far], [(wide - 1, 0), (wide - 1, half_rows)])

        given = swap(done[far][1])
        back = total(done[far][0], given).astype(BF16)
        back, *_ = both(back, *out_blocks, *handed)
        to_above, to_below = both(up(back[:half_rows]), down(back[half_rows:]))
        for _ in range(early + 1, far):
            out_step()
        for d in range(far - 1, 0, -1):
            if d not in done:
                done[d] = expert(pairs[d], [(2 * d - 1, 0), (2 * d, 0)], given)
            given = swap(done[d][1])
            below = total(done[d][0][:rows], given[:rows])
            above = total(done[d][0][rows:], given[rows:])
            if d == far - 1:
                above = jnp.concatenate(
                    [above[:half_rows] + to_above.astype(F32), above[half_rows:]], axis=0
                )
                below = jnp.concatenate(
                    [below[:half_rows], below[half_rows:] + to_below.astype(F32)], axis=0
                )
            else:
                above, below = above + to_above.astype(F32), below + to_below.astype(F32)
            above, below = above.astype(BF16), below.astype(BF16)
            if d == far - 1:
                above, below = after((above, below), *out_blocks)
                hand(len(handed), 2)
            elif d == far - 2:
                above, below = after((above, below), *handed)
                hand(len(handed), len(out_blocks) - len(handed))
            else:
                above, below = after((above, below), *handed)
            to_above, to_below = both(up(above), down(below))
        mixture = total(done[0][0], swap(done[0][1]), to_above)
        mixture = (mixture + to_below.astype(F32)).astype(BF16)
        return kernel_call(
            functools.partial(final_body, out_depth),
            shape(rows, columns),
            4,
            2 * rows * width * columns,
            2 * width * columns + 4 * rows * columns,
            [
                pltpu.VMEM((rows, width), BF16),
                pltpu.VMEM((width, columns), BF16),
                pltpu.SemaphoreType.DMA((1 + 2 * len(out_blocks),)),
            ],
            1 + 2 * len(out_blocks),
            BIG,
        )(
            info.at[1].set(side.astype(jnp.int32)),
            kept,
            mixture,
            swap(mixture),
            w_out,
            *out_blocks,
            *handed,
        )

    return local


def solution(mesh):
    in_specs = (
        P(("groups", "wide"), None),
        P(),
        P("wide", None),
        P("wide", "narrow"),
        P("wide", None, "narrow"),
        P("wide", "narrow", None),
        P(("groups", "wide"), None),
        P(("groups", "wide"), None),
    )
    out_specs = P(("groups", "wide"), "narrow")
    local = make_local(ring_order(mesh))
    return jax.shard_map(
        local, mesh=mesh, in_specs=in_specs, out_specs=out_specs, check_vma=False
    )
```

```python
import functools

import jax
import jax.numpy as jnp
from jax import lax
from jax.experimental import pallas as pl
from jax.experimental.pallas import tpu as pltpu
from jax.sharding import PartitionSpec as P

F32, BF16 = jnp.float32, jnp.bfloat16
VMEM = pl.BlockSpec(memory_space=pltpu.VMEM)
SMEM = pl.BlockSpec(memory_space=pltpu.SMEM)
ANY = pl.BlockSpec(memory_space=pl.ANY)
LIMIT, BIG = 20 * 2**20, 20 * 2**20


def kernel_call(body, out, n_in, flops, nbytes, scratch=(), n_any=0, limit=LIMIT):
    return pl.pallas_call(
        body,
        out_shape=out,
        in_specs=[SMEM] + [VMEM] * (n_in - 1) + [ANY] * n_any,
        out_specs=jax.tree.map(lambda _: VMEM, out),
        scratch_shapes=list(scratch),
        compiler_params=pltpu.CompilerParams(vmem_limit_bytes=limit),
        cost_estimate=pl.CostEstimate(
            flops=flops, bytes_accessed=nbytes, transcendentals=0
        ),
    )


def norm_body(info, tokens, gain, out):
    rows, model = tokens.shape
    step = 16

    @pl.loop(0, rows // step)
    def _(i):
        at = pl.ds(pl.multiple_of(i * step, step), step)
        x = tokens[at, :].astype(F32)
        mean = jnp.sum(x * x, axis=1, keepdims=True) * (1.0 / model)
        x = tokens[at, :].astype(F32) * lax.rsqrt(mean + 1e-05) * gain[...]
        out[at, :] = x.astype(BF16)


def fetch(sources, places, done):
    copies = [
        pltpu.make_async_copy(a, b, done.at[i])
        for i, (a, b) in enumerate(zip(sources, places))
    ]
    for copy in copies:
        copy.start()

    def arrived(i):
        copies[i].wait()
        return places[i]

    return arrived


def places_for(arrays):
    return [pltpu.VMEM(a.shape, a.dtype) for a in arrays] + [
        pltpu.SemaphoreType.DMA((len(arrays),))
    ]


def start_body(wide, info, ids, weights, tokens, w_in, raw, block, done):
    rows, depth, quarter = raw.shape[0], w_in.shape[0], block.shape[1]
    columns = pl.ds(pl.multiple_of(info[1] * quarter, quarter), quarter)
    parts = done.shape[0] // 2
    copies = []
    for i in range(parts):
        size = rows // parts
        at = pl.ds(pl.multiple_of(info[0] * rows + i * size, size), size)
        to = raw.at[pl.ds(i * size, size), :]
        copies.append(pltpu.make_async_copy(tokens.at[at, :], to, done.at[i]))
        at = pl.ds(i * (depth // parts), depth // parts)
        copies.append(
            pltpu.make_async_copy(w_in.at[at, columns], block.at[at, :], done.at[parts + i])
        )
    for copy in copies:
        copy.start()
    number = lax.broadcasted_iota(jnp.int32, (wide, ids.shape[1]), 0)
    dense = jnp.zeros(number.shape, F32)
    for k in range(ids.shape[0]):
        dense += jnp.where(ids[k : k + 1, :] == number, weights[k : k + 1, :], 0.0)
    terms = []
    for _ in range(3):
        terms.append(dense.astype(BF16).astype(F32))
        dense = dense - terms[-1]
    empty = block.shape[0] - depth - 3 * wide
    if empty:
        terms.append(jnp.zeros((empty, ids.shape[1]), F32))
    block[depth:, :] = jnp.concatenate(terms, axis=0).astype(BF16)
    for copy in copies:
        copy.wait()


def pack_body(info, first, second, out, done):
    size = first.shape[0]
    places = [out.at[pl.ds(0, size), :], out.at[pl.ds(size, second.shape[0]), :]]
    arrived = fetch([first, second], places, done)
    arrived(0), arrived(1)


def near_body(depth, n, info, *refs):
    lefts, rest = refs[:n], refs[n:]
    count = (len(rest) - 3) // 2
    blocks, out, columns = rest[:count], rest[count], rest[count + 1]
    places, done = rest[count + 2 : -1], rest[-1]
    arrived = fetch(blocks, places, done)
    total = None
    for i in range(count):
        at = pl.ds(pl.multiple_of(info[2 + i] * depth, depth), depth)
        left = jnp.concatenate([a[:, at] for a in lefts], axis=0)
        term = jnp.dot(left, arrived(i)[:depth, :], preferred_element_type=F32)
        total = term if total is None else total + term
    out[...] = total
    at = pl.ds(pl.multiple_of(info[2 + count] * depth, depth), depth)
    columns[...] = jnp.concatenate([a[:, at] for a in lefts], axis=0)


def far_body(depth, info, partial, left, low, high, out):
    right = jnp.concatenate([low[: depth // 2, :], high[: depth // 2, :]], axis=0)
    total = jnp.dot(left[...], right, preferred_element_type=F32) + partial[...]
    total = total.astype(BF16)
    core, half = info[0], total.shape[0] // 2
    out[pl.ds(pl.multiple_of(core * half, half), half), :] = total[:half]
    out[pl.ds(pl.multiple_of((1 - core) * half, half), half), :] = total[half:]


def mine_body(depth, wide, first, info, normed, *refs):
    refs, (out, gates) = list(refs[:-2]), refs[-2:]
    total = lines = None
    if first:
        total, lines = refs.pop()[...], refs.pop()[...]
    other = refs.pop() if first == wide - 1 else None
    extra = -(-3 * wide // 16) * 16
    number = lax.broadcasted_iota(jnp.int32, (extra, refs[0].shape[1]), 0)
    chosen = (number % wide == info[1]) & (number < 3 * wide)
    i = first
    while refs:
        block = refs.pop(0)
        if i < wide - 1:
            right, carried = block[:depth, :], block[depth:, :]
        else:
            high = refs.pop(0)
            right = [block[...], high[: depth // 2, :]]
            right, carried = jnp.concatenate(right, axis=0), high[depth // 2 :, :]
        at = pl.ds(pl.multiple_of(info[2 + i] * depth, depth), depth)
        term = jnp.dot(normed[:, at], right, preferred_element_type=F32)
        total = term if total is None else total + term
        line = jnp.where(chosen, carried.astype(F32), 0.0)
        line = jnp.sum(line, axis=0, keepdims=True)
        lines = line if lines is None else jnp.concatenate([lines, line], axis=0)
        i += 1
    if other is None:
        out[...] = total
        gates[...] = lines
        return
    size = total.shape[1]
    side = info[2 + wide]
    out[:, pl.ds(pl.multiple_of(side * size, size), size)] = total.astype(BF16)
    out[:, pl.ds(pl.multiple_of((1 - side) * size, size), size)] = other[...]
    gates[...] = lines.T


def expert_body(columns, info, *refs):
    n = len(columns)
    own, other = refs[:n], refs[n : 2 * n]
    gates, up, down, stay, give, x, total = refs[2 * n :]
    core = info[0]
    half = own[0].shape[1]
    here = pl.ds(pl.multiple_of(core * half, half), half)
    there = pl.ds(pl.multiple_of((1 - core) * half, half), half)
    begin = 0
    for a, b in zip(own, other):
        size = a.shape[0]
        x[begin : begin + size, here] = a[...]
        x[begin : begin + size, there] = b[...]
        begin += size
    hidden = up.shape[0]
    chunk = max(c for c in range(16, 513, 16) if hidden % c == 0)
    for i in range(hidden // chunk):
        at = slice(i * chunk, (i + 1) * chunk)
        h = lax.dot_general(
            x[...], up[at, :], (((1,), (1,)), ((), ())), preferred_element_type=F32
        )
        h = jnp.square(jnp.maximum(h, 0.0)).astype(BF16)
        part = jnp.dot(h, down[at, :], preferred_element_type=F32)
        if i == 0:
            total[...] = part
        else:
            total[...] += part
    begin = 0
    for j, (column, first) in enumerate(columns):
        size = own[j].shape[0]
        gate = gates[first : first + size, column : column + 1]
        rows = slice(begin, begin + size)
        stay[rows, :] = (total[rows, here] * gate).astype(BF16)
        give[rows, :] = (total[rows, there] * gate).astype(BF16)
        begin += size


def final_body(depth, info, kept, mine, back, *rest):
    *blocks, out, mixture, full, done = rest
    core, side, me = info[0], info[1], info[2]
    count = (len(blocks) - 1) * 2 // 3
    pairs = [(b, b.shape[0] // 2) for b in blocks[1 + count :]]
    blocks = blocks[: 1 + count] + [
        b.at[pl.ds(i * size, size), :] for b, size in pairs for i in range(2)
    ]
    span = blocks[1].shape[1]
    places = [full.at[pl.ds(pl.multiple_of(me * depth, depth), depth), :]]
    for number in range(2):
        at = pl.ds(pl.multiple_of((side + number) % 2 * span, span), span)
        for i in range(count):
            size = blocks[1 + i].shape[0]
            begin = info[2 + min(1 + i, count - 1)] * depth
            if i == count - 1:
                begin = begin + size
            places.append(full.at[pl.ds(pl.multiple_of(begin, size), size), at])
    arrived = fetch(blocks, places, done)
    half = mine.shape[1]
    mixture[:, pl.ds(pl.multiple_of(core * half, half), half)] = mine[...]
    mixture[:, pl.ds(pl.multiple_of((1 - core) * half, half), half)] = back[...]
    for i in range(len(blocks)):
        arrived(i)
    step = 512
    for i in range(full.shape[1] // step):
        at = slice(i * step, (i + 1) * step)
        branch = jnp.dot(mixture[...], full[:, at], preferred_element_type=F32)
        out[:, at] = (kept[:, at].astype(F32) + branch).astype(BF16)


def after(x, *others):
    return lax.optimization_barrier((x, others))[0]


def both(*xs):
    return lax.optimization_barrier(xs)


def ring_order(mesh):
    wide = mesh.shape["wide"]
    line = mesh.devices.reshape(-1, wide, mesh.shape["narrow"])[0, :, 0]
    places = [tuple(getattr(d, "coords", (0,))) for d in line]
    spread = [len(set(c)) for c in zip(*places)]
    if sum(s > 1 for s in spread) == 2 and wide % 2 == 0:
        return list(range(0, wide, 2)) + list(range(wide - 1, 0, -2))
    return list(range(wide))


def make_local(order):
    wide = len(order)
    far = wide // 2
    up_perm = [(order[i], order[(i + 1) % wide]) for i in range(wide)]
    down_perm = [(order[(i + 1) % wide], order[i]) for i in range(wide)]
    offsets = [0] + [s * d for d in range(1, far) for s in (-1, 1)] + [far]
    sources = [[order[(order.index(i) + o) % wide] for o in offsets] for i in range(wide)]

    def local(tokens, norm_gain, w_in, w_out, w_up, w_down, expert_ids, gate_weights):
        groups = lax.axis_size("groups")
        side = lax.axis_index("groups") % 2
        me = lax.axis_index("wide")
        core = lax.axis_index("narrow")
        rows, model = tokens.shape
        half_rows = rows // 2
        depth, width = w_in.shape
        half, quarter = width // 2, width // 4
        info = jnp.concatenate(
            [
                jnp.stack([core, me]),
                jnp.asarray(sources, jnp.int32)[me],
                side.reshape(1),
            ]
        ).astype(jnp.int32)

        def up(x):
            return lax.ppermute(x, "wide", up_perm)

        def down(x):
            return lax.ppermute(x, "wide", down_perm)

        def swap(x):
            return lax.ppermute(x, "narrow", [(0, 1), (1, 0)])

        def across(x):
            return lax.ppermute(x, "groups", [(i, i ^ 1) for i in range(groups)])

        def shape(*dims, kind=BF16):
            return jax.ShapeDtypeStruct(dims, kind)

        columns = w_out.shape[1]
        out_half = lax.dynamic_slice_in_dim(
            w_out, side * (columns // 2), columns // 2, 1
        )
        out_depth = w_out.shape[0]
        out_blocks = []
        out_below = out_above = out_half

        def out_step(*others, beside=()):
            nonlocal out_below, out_above
            out_below, out_above = after((out_below, out_above), *others)
            if len(out_blocks) == 2 * far - 2:
                cut = out_depth // 2
                out_below, out_above = out_below[:cut], out_above[cut:]
            moved = both(up(out_below), down(out_above), *beside)
            out_below, out_above = moved[:2]
            out_blocks.extend([out_below, out_above])

        handed = []

        packs = []

        def pack(*others):
            pair = out_blocks[2 * len(packs) :][:2]
            out = shape(2 * pair[0].shape[0], pair[0].shape[1])
            one = kernel_call(
                pack_body,
                out,
                1,
                out.size,
                4 * out.size,
                [pltpu.SemaphoreType.DMA((2,))],
                2,
            )(after(info, *others), *pair)
            packs.append(one)
            return [one]

        def hand(*others):
            handed.append(across(after(packs[len(handed)], *others)))

        out_step()

        extra = -(-3 * wide // 16) * 16
        raw, block = pl.pallas_call(
            functools.partial(start_body, wide),
            out_shape=(shape(half_rows, model), shape(depth + extra, quarter)),
            in_specs=[SMEM, VMEM, VMEM, ANY, ANY],
            out_specs=(VMEM, VMEM),
            scratch_shapes=[pltpu.SemaphoreType.DMA((8,))],
        )(
            jnp.stack([core, core * 2 + side]).astype(jnp.int32),
            expert_ids.T,
            gate_weights.T,
            tokens,
            w_in,
        )
        block = after(block, *out_blocks)

        def norm(x, *others):
            return kernel_call(
                norm_body,
                shape(*x.shape),
                3,
                8 * x.size,
                4 * x.size,
            )(after(info, *others), x, norm_gain.reshape(1, model))

        def step(below, above, *beside):
            return both(up(below), down(above), *beside)[:2]

        first = across(raw)
        flops = 2 * rows * model * quarter
        nbytes = 2 * (rows * model + model * quarter)

        def near(*lefts):
            return kernel_call(
                functools.partial(near_body, depth, len(lefts)),
                (shape(rows, quarter, kind=F32), shape(rows, depth)),
                1 + len(lefts),
                flops,
                nbytes,
                places_for(blocks),
                len(blocks),
                BIG,
            )(info, *lefts, *blocks)

        def mine(first, part, *before, others=()):
            last = first + len(part) > wide
            outs = shape(rows, half) if last else shape(rows, quarter, kind=F32)
            number = min(first + len(part), wide)
            lines = shape(rows, wide, kind=F32) if last else shape(number, rows, kind=F32)
            return kernel_call(
                functools.partial(mine_body, depth, wide, first),
                (outs, lines),
                2 + len(part) + len(before),
                flops * len(part) // wide,
                nbytes * len(part) // wide,
            )(after(info, *others), normed, *part, *before)

        blocks = [block]
        below = above = block
        lat_mine = []
        for d in range(1, far):
            beside = []
            if d == 1:
                normed = norm(tokens, block)
                beside = [normed]
            else:
                begin = 0 if d == 2 else 2 * d - 3
                lat_mine = mine(begin, blocks[begin:], *lat_mine[::-1])
                beside = [*lat_mine]
            if d == 2:
                kept = lax.dynamic_slice_in_dim(
                    after(tokens, below), core * columns, columns, 1
                )
                beside += [kept, *pack(below)]
            elif d == 3:
                first = norm(first, below)
                beside += [first]
            below, above = step(below, above, *beside)
            blocks += [below, above]
        second = swap(after(first, below))
        near_there = near(first, second)
        begin = len(blocks) - 2
        lat_mine = mine(begin, blocks[begin:], *lat_mine[::-1])
        ends = step(below[: depth // 2], above[depth // 2 :], *near_there, *lat_mine)

        lat_there = kernel_call(
            functools.partial(far_body, depth),
            shape(rows, quarter),
            5,
            flops // wide,
            nbytes // wide,
        )(info, *near_there, *ends)
        lat_other = across(lat_there)
        out_step(lat_there)
        latent, gates = mine(len(blocks), ends, lat_other, *lat_mine[::-1])
        up_weight, down_weight = w_up[0].T, w_down[0]
        hidden = up_weight.shape[0]

        def expert(xs, columns, *others, swapped=None):
            size = sum(x.shape[0] for x in xs)
            out = shape(size, half)
            ys = swapped or [swap(x) for x in xs]
            return kernel_call(
                functools.partial(expert_body, columns),
                (out, out),
                4 + 2 * len(xs),
                4 * size * width * hidden,
                4 * hidden * width + 4 * size * width,
                [pltpu.VMEM((size, width), BF16), pltpu.VMEM((size, width), F32)],
            )(after(info, *others), *xs, *ys, gates, up_weight, down_weight)

        def total(stay, given, more=None):
            t = stay.astype(F32) + given.astype(F32)
            return t if more is None else t + more.astype(F32)

        done = {}
        pairs = [(latent, latent)]
        for d in range(1, far + 1):
            below, above = pairs[-1]
            beside = []
            if d == 1:
                swapped = swap(latent)
                beside = [*out_blocks, swapped]
                hand(latent)
            elif d == 2:
                beside = [*pack(below), *handed]
                hand()
            elif d == 3:
                done[1] = expert(pairs[1], [(1, 0), (2, 0)], below)
                beside = [*done[1], *handed]
            if d == far:
                done[d - 1] = expert(pairs[d - 1], [(2 * d - 3, 0), (2 * d - 2, 0)])
                beside = [*done[d - 1]]
                below, above = below[:half_rows], above[half_rows:]
            pairs.append(step(below, above, *beside))
        below, above = pairs[far]
        done[far] = expert([below, above], [(wide - 1, 0), (wide - 1, half_rows)])

        given = swap(done[far][1])
        back = total(done[far][0], given).astype(BF16)
        out_step(*pairs[far])
        back = after(back, *out_blocks)
        done[far - 2] = expert(
            pairs[far - 2], [(2 * far - 5, 0), (2 * far - 4, 0)], back
        )
        beside = [*done[far - 2], *pack(back)]
        out_step(back)
        to_above, to_below = step(
            back[:half_rows], back[half_rows:], *beside, *out_blocks
        )
        for d in range(far - 1, 0, -1):
            given = swap(done[d][1])
            below = total(done[d][0][:rows], given[:rows])
            above = total(done[d][0][rows:], given[rows:])
            if d == far - 1:
                above = jnp.concatenate(
                    [above[:half_rows] + to_above.astype(F32), above[half_rows:]], axis=0
                )
                below = jnp.concatenate(
                    [below[:half_rows], below[half_rows:] + to_below.astype(F32)], axis=0
                )
            else:
                above, below = above + to_above.astype(F32), below + to_below.astype(F32)
            above, below = above.astype(BF16), below.astype(BF16)
            beside = []
            if d > 1 and d - 1 not in done:
                done[d - 1] = expert(
                    pairs[d - 1], [(2 * d - 3, 0), (2 * d - 2, 0)], to_above, to_below
                )
                beside += done[d - 1]
            if d == 2:
                done[0] = expert(
                    [latent], [(0, 0)], to_above, to_below, swapped=[swapped]
                )
                beside += done[0]
            if d == 1:
                given0 = swap(done[0][1])
                beside += [given0]
            if len(out_blocks) < 2 * far:
                out_step(to_above, to_below)
                beside += out_blocks
            if len(packs) < far:
                beside += pack(to_above)
            beside += handed[2:]
            if len(handed) < far:
                hand(to_above)
            to_above, to_below = step(above, below, *beside)
        mixture = total(done[0][0], given0, to_above)
        mixture = (mixture + to_below.astype(F32)).astype(BF16)
        return kernel_call(
            functools.partial(final_body, out_depth),
            shape(rows, columns),
            4,
            2 * rows * width * columns,
            2 * width * columns + 4 * rows * columns,
            [
                pltpu.VMEM((rows, width), BF16),
                pltpu.VMEM((width, columns), BF16),
                pltpu.SemaphoreType.DMA((1 + 2 * len(out_blocks),)),
            ],
            1 + len(out_blocks) + len(handed),
            BIG,
        )(
            info.at[1].set(side.astype(jnp.int32)),
            kept,
            mixture,
            swap(mixture),
            w_out,
            *out_blocks,
            *handed,
        )

    return local


def solution(mesh):
    in_specs = (
        P(("groups", "wide"), None),
        P(),
        P("wide", None),
        P("wide", "narrow"),
        P("wide", None, "narrow"),
        P("wide", "narrow", None),
        P(("groups", "wide"), None),
        P(("groups", "wide"), None),
    )
    out_specs = P(("groups", "wide"), "narrow")
    local = make_local(ring_order(mesh))
    return jax.shard_map(
        local, mesh=mesh, in_specs=in_specs, out_specs=out_specs, check_vma=False
    )
```

```python
import functools

import jax
import jax.numpy as jnp
from jax import lax
from jax.experimental import pallas as pl
from jax.experimental.pallas import tpu as pltpu
from jax.sharding import PartitionSpec as P

F32, BF16 = jnp.float32, jnp.bfloat16
VMEM = pl.BlockSpec(memory_space=pltpu.VMEM)
SMEM = pl.BlockSpec(memory_space=pltpu.SMEM)
ANY = pl.BlockSpec(memory_space=pl.ANY)
LIMIT, BIG = 20 * 2**20, 20 * 2**20


def kernel_call(body, out, n_in, flops, nbytes, scratch=(), n_any=0, limit=LIMIT):
    return pl.pallas_call(
        body,
        out_shape=out,
        in_specs=[SMEM] + [VMEM] * (n_in - 1) + [ANY] * n_any,
        out_specs=jax.tree.map(lambda _: VMEM, out),
        scratch_shapes=list(scratch),
        compiler_params=pltpu.CompilerParams(vmem_limit_bytes=limit),
        cost_estimate=pl.CostEstimate(
            flops=flops, bytes_accessed=nbytes, transcendentals=0
        ),
    )


def norm_body(info, tokens, gain, out):
    rows, model = tokens.shape
    step = 16

    @pl.loop(0, rows // step)
    def _(i):
        at = pl.ds(pl.multiple_of(i * step, step), step)
        x = tokens[at, :].astype(F32)
        mean = jnp.sum(x * x, axis=1, keepdims=True) * (1.0 / model)
        x = tokens[at, :].astype(F32) * lax.rsqrt(mean + 1e-05) * gain[...]
        out[at, :] = x.astype(BF16)


def fetch(sources, places, done):
    copies = [
        pltpu.make_async_copy(a, b, done.at[i])
        for i, (a, b) in enumerate(zip(sources, places))
    ]
    for copy in copies:
        copy.start()

    def arrived(i):
        copies[i].wait()
        return places[i]

    return arrived


def places_for(arrays):
    return [pltpu.VMEM(a.shape, a.dtype) for a in arrays] + [
        pltpu.SemaphoreType.DMA((len(arrays),))
    ]


def start_body(wide, info, ids, weights, tokens, w_in, raw, block, done):
    rows, depth, quarter = raw.shape[0], w_in.shape[0], block.shape[1]
    columns = pl.ds(pl.multiple_of(info[1] * quarter, quarter), quarter)
    parts = done.shape[0] // 2
    copies = []
    for i in range(parts):
        size = rows // parts
        at = pl.ds(pl.multiple_of(info[0] * rows + i * size, size), size)
        to = raw.at[pl.ds(i * size, size), :]
        copies.append(pltpu.make_async_copy(tokens.at[at, :], to, done.at[i]))
        at = pl.ds(i * (depth // parts), depth // parts)
        copies.append(
            pltpu.make_async_copy(w_in.at[at, columns], block.at[at, :], done.at[parts + i])
        )
    for copy in copies:
        copy.start()
    number = lax.broadcasted_iota(jnp.int32, (wide, ids.shape[1]), 0)
    dense = jnp.zeros(number.shape, F32)
    for k in range(ids.shape[0]):
        dense += jnp.where(ids[k : k + 1, :] == number, weights[k : k + 1, :], 0.0)
    terms = []
    for _ in range(3):
        terms.append(dense.astype(BF16).astype(F32))
        dense = dense - terms[-1]
    empty = block.shape[0] - depth - 3 * wide
    if empty:
        terms.append(jnp.zeros((empty, ids.shape[1]), F32))
    block[depth:, :] = jnp.concatenate(terms, axis=0).astype(BF16)
    for copy in copies:
        copy.wait()


def pack_body(info, first, second, out, done):
    size = first.shape[0]
    places = [out.at[pl.ds(0, size), :], out.at[pl.ds(size, second.shape[0]), :]]
    arrived = fetch([first, second], places, done)
    arrived(0), arrived(1)


def near_body(depth, n, info, *refs):
    lefts, rest = refs[:n], refs[n:]
    count = (len(rest) - 3) // 2
    blocks, out, columns = rest[:count], rest[count], rest[count + 1]
    places, done = rest[count + 2 : -1], rest[-1]
    arrived = fetch(blocks, places, done)
    total = None
    for i in range(count):
        at = pl.ds(pl.multiple_of(info[2 + i] * depth, depth), depth)
        left = jnp.concatenate([a[:, at] for a in lefts], axis=0)
        term = jnp.dot(left, arrived(i)[:depth, :], preferred_element_type=F32)
        total = term if total is None else total + term
    out[...] = total
    at = pl.ds(pl.multiple_of(info[2 + count] * depth, depth), depth)
    columns[...] = jnp.concatenate([a[:, at] for a in lefts], axis=0)


def far_body(depth, info, partial, left, low, high, out):
    right = jnp.concatenate([low[: depth // 2, :], high[: depth // 2, :]], axis=0)
    total = jnp.dot(left[...], right, preferred_element_type=F32) + partial[...]
    total = total.astype(BF16)
    core, half = info[0], total.shape[0] // 2
    out[pl.ds(pl.multiple_of(core * half, half), half), :] = total[:half]
    out[pl.ds(pl.multiple_of((1 - core) * half, half), half), :] = total[half:]


def mine_body(depth, wide, first, info, normed, *refs):
    refs, (out, gates) = list(refs[:-2]), refs[-2:]
    total = lines = None
    if first:
        total, lines = refs.pop()[...], refs.pop()[...]
    other = refs.pop() if first == wide - 1 else None
    extra = -(-3 * wide // 16) * 16
    number = lax.broadcasted_iota(jnp.int32, (extra, refs[0].shape[1]), 0)
    chosen = (number % wide == info[1]) & (number < 3 * wide)
    i = first
    while refs:
        block = refs.pop(0)
        if i < wide - 1:
            right, carried = block[:depth, :], block[depth:, :]
        else:
            high = refs.pop(0)
            right = [block[...], high[: depth // 2, :]]
            right, carried = jnp.concatenate(right, axis=0), high[depth // 2 :, :]
        at = pl.ds(pl.multiple_of(info[2 + i] * depth, depth), depth)
        term = jnp.dot(normed[:, at], right, preferred_element_type=F32)
        total = term if total is None else total + term
        line = jnp.where(chosen, carried.astype(F32), 0.0)
        line = jnp.sum(line, axis=0, keepdims=True)
        lines = line if lines is None else jnp.concatenate([lines, line], axis=0)
        i += 1
    if other is None:
        out[...] = total
        gates[...] = lines
        return
    size = total.shape[1]
    side = info[2 + wide]
    out[:, pl.ds(pl.multiple_of(side * size, size), size)] = total.astype(BF16)
    out[:, pl.ds(pl.multiple_of((1 - side) * size, size), size)] = other[...]
    gates[...] = lines.T


def expert_body(columns, info, *refs):
    n = len(columns)
    own, other = refs[:n], refs[n : 2 * n]
    gates, up, down, stay, give, x, hid = refs[2 * n :]
    core = info[0]
    half = own[0].shape[1]
    here = pl.ds(pl.multiple_of(core * half, half), half)
    there = pl.ds(pl.multiple_of((1 - core) * half, half), half)
    begin = 0
    for a, b in zip(own, other):
        size = a.shape[0]
        x[begin : begin + size, here] = a[...]
        x[begin : begin + size, there] = b[...]
        begin += size
    hidden = up.shape[0]
    chunk = hidden if hidden % 128 else max(c for c in range(128, 513, 128) if hidden % c == 0)
    for i in range(hidden // chunk):
        at = slice(i * chunk, (i + 1) * chunk)
        h = lax.dot_general(
            x[...], up[at, :], (((1,), (1,)), ((), ())), preferred_element_type=F32
        )
        hid[:, at] = jnp.square(jnp.maximum(h, 0.0)).astype(BF16)
    for columns_at, out in ((here, stay), (there, give)):
        total = jnp.dot(hid[...], down[:, columns_at], preferred_element_type=F32)
        begin = 0
        for j, (column, first) in enumerate(columns):
            size = own[j].shape[0]
            gate = gates[first : first + size, column : column + 1]
            rows = slice(begin, begin + size)
            out[rows, :] = (total[rows] * gate).astype(BF16)
            begin += size


def assemble_body(depth, info, *rest):
    *blocks, full, done = rest
    side, me = info[1], info[2]
    count = (len(blocks) - 1) * 2 // 3
    pairs = [(b, b.shape[0] // 2) for b in blocks[1 + count :]]
    blocks = blocks[: 1 + count] + [
        b.at[pl.ds(i * size, size), :] for b, size in pairs for i in range(2)
    ]
    span = blocks[1].shape[1]
    places = [full.at[pl.ds(pl.multiple_of(me * depth, depth), depth), :]]
    for number in range(2):
        at = pl.ds(pl.multiple_of((side + number) % 2 * span, span), span)
        for i in range(count):
            size = blocks[1 + i].shape[0]
            begin = info[2 + min(1 + i, count - 1)] * depth
            if i == count - 1:
                begin = begin + size
            places.append(full.at[pl.ds(pl.multiple_of(begin, size), size), at])
    arrived = fetch(blocks, places, done)
    for i in range(len(blocks)):
        arrived(i)


def final_body(info, kept, mine, back, full, out, mixture):
    core, half = info[0], mine.shape[1]
    mixture[:, pl.ds(pl.multiple_of(core * half, half), half)] = mine[...]
    mixture[:, pl.ds(pl.multiple_of((1 - core) * half, half), half)] = back[...]
    step = 512
    for i in range(full.shape[1] // step):
        at = slice(i * step, (i + 1) * step)
        branch = jnp.dot(mixture[...], full[:, at], preferred_element_type=F32)
        out[:, at] = (kept[:, at].astype(F32) + branch).astype(BF16)


def after(x, *others):
    return lax.optimization_barrier((x, others))[0]


def both(*xs):
    return lax.optimization_barrier(xs)


def ring_order(mesh):
    wide = mesh.shape["wide"]
    line = mesh.devices.reshape(-1, wide, mesh.shape["narrow"])[0, :, 0]
    places = [tuple(getattr(d, "coords", (0,))) for d in line]
    spread = [len(set(c)) for c in zip(*places)]
    if sum(s > 1 for s in spread) == 2 and wide % 2 == 0:
        return list(range(0, wide, 2)) + list(range(wide - 1, 0, -2))
    return list(range(wide))


def make_local(order):
    wide = len(order)
    far = wide // 2
    up_perm = [(order[i], order[(i + 1) % wide]) for i in range(wide)]
    down_perm = [(order[(i + 1) % wide], order[i]) for i in range(wide)]
    offsets = [0] + [s * d for d in range(1, far) for s in (-1, 1)] + [far]
    sources = [[order[(order.index(i) + o) % wide] for o in offsets] for i in range(wide)]

    def local(tokens, norm_gain, w_in, w_out, w_up, w_down, expert_ids, gate_weights):
        groups = lax.axis_size("groups")
        side = lax.axis_index("groups") % 2
        me = lax.axis_index("wide")
        core = lax.axis_index("narrow")
        rows, model = tokens.shape
        half_rows = rows // 2
        depth, width = w_in.shape
        half, quarter = width // 2, width // 4
        info = jnp.concatenate(
            [
                jnp.stack([core, me]),
                jnp.asarray(sources, jnp.int32)[me],
                side.reshape(1),
            ]
        ).astype(jnp.int32)

        def up(x):
            return lax.ppermute(x, "wide", up_perm)

        def down(x):
            return lax.ppermute(x, "wide", down_perm)

        def swap(x):
            return lax.ppermute(x, "narrow", [(0, 1), (1, 0)])

        def across(x):
            return lax.ppermute(x, "groups", [(i, i ^ 1) for i in range(groups)])

        def shape(*dims, kind=BF16):
            return jax.ShapeDtypeStruct(dims, kind)

        columns = w_out.shape[1]
        out_half = lax.dynamic_slice_in_dim(
            w_out, side * (columns // 2), columns // 2, 1
        )
        out_depth = w_out.shape[0]
        out_blocks = []
        out_below = out_above = out_half

        def out_step(*others, beside=()):
            nonlocal out_below, out_above
            out_below, out_above = after((out_below, out_above), *others)
            if len(out_blocks) == 2 * far - 2:
                cut = out_depth // 2
                out_below, out_above = out_below[:cut], out_above[cut:]
            moved = both(up(out_below), down(out_above), *beside)
            out_below, out_above = moved[:2]
            out_blocks.extend([out_below, out_above])

        handed = []

        packs = []

        def pack(*others):
            pair = out_blocks[2 * len(packs) :][:2]
            out = shape(2 * pair[0].shape[0], pair[0].shape[1])
            one = kernel_call(
                pack_body,
                out,
                1,
                out.size,
                4 * out.size,
                [pltpu.SemaphoreType.DMA((2,))],
                2,
            )(after(info, *others), *pair)
            packs.append(one)
            return [one]

        def hand(*others):
            handed.append(across(after(packs[len(handed)], *others)))

        out_step()

        extra = -(-3 * wide // 16) * 16
        raw, block = pl.pallas_call(
            functools.partial(start_body, wide),
            out_shape=(shape(half_rows, model), shape(depth + extra, quarter)),
            in_specs=[SMEM, VMEM, VMEM, ANY, ANY],
            out_specs=(VMEM, VMEM),
            scratch_shapes=[pltpu.SemaphoreType.DMA((8,))],
        )(
            jnp.stack([core, core * 2 + side]).astype(jnp.int32),
            expert_ids.T,
            gate_weights.T,
            tokens,
            w_in,
        )

        def norm(x, *others):
            return kernel_call(
                norm_body,
                shape(*x.shape),
                3,
                8 * x.size,
                4 * x.size,
            )(after(info, *others), x, norm_gain.reshape(1, model))

        def step(below, above, *beside):
            return both(up(below), down(above), *beside)[:2]

        first = across(raw)
        flops = 2 * rows * model * quarter
        nbytes = 2 * (rows * model + model * quarter)

        def near(*lefts):
            return kernel_call(
                functools.partial(near_body, depth, len(lefts)),
                (shape(rows, quarter, kind=F32), shape(rows, depth)),
                1 + len(lefts),
                flops,
                nbytes,
                places_for(blocks),
                len(blocks),
                BIG,
            )(info, *lefts, *blocks)

        def mine(first, part, *before, others=()):
            last = first + len(part) > wide
            outs = shape(rows, half) if last else shape(rows, quarter, kind=F32)
            number = min(first + len(part), wide)
            lines = shape(rows, wide, kind=F32) if last else shape(number, rows, kind=F32)
            return kernel_call(
                functools.partial(mine_body, depth, wide, first),
                (outs, lines),
                2 + len(part) + len(before),
                flops * len(part) // wide,
                nbytes * len(part) // wide,
            )(after(info, *others), normed, *part, *before)

        blocks = [block]
        below = above = block
        lat_mine = []
        for d in range(1, far):
            beside = []
            if d == 1:
                normed = norm(tokens, block)
                beside = [normed]
            else:
                begin = 0 if d == 2 else 2 * d - 3
                lat_mine = mine(begin, blocks[begin:], *lat_mine[::-1])
                beside = [*lat_mine]
            if d == 2:
                kept = lax.dynamic_slice_in_dim(
                    after(tokens, below), core * columns, columns, 1
                )
                beside += [kept, *pack(below)]
            elif d == 3:
                first = norm(first, below)
                beside += [first]
            below, above = step(below, above, *beside)
            blocks += [below, above]
        second = swap(after(first, below))
        near_there = near(first, second)
        begin = len(blocks) - 2
        lat_mine = mine(begin, blocks[begin:], *lat_mine[::-1])
        ends = step(below[: depth // 2], above[depth // 2 :], *near_there, *lat_mine)

        lat_there = kernel_call(
            functools.partial(far_body, depth),
            shape(rows, quarter),
            5,
            flops // wide,
            nbytes // wide,
        )(info, *near_there, *ends)
        lat_other = across(lat_there)
        out_step(lat_there)
        latent, gates = mine(len(blocks), ends, lat_other, *lat_mine[::-1])
        side_info = info.at[1].set(side.astype(jnp.int32))
        up_weight, down_weight = w_up[0].T, w_down[0]
        hidden = up_weight.shape[0]

        def expert(xs, columns, *others, swapped=None):
            size = sum(x.shape[0] for x in xs)
            out = shape(size, half)
            ys = swapped or [swap(x) for x in xs]
            return kernel_call(
                functools.partial(expert_body, columns),
                (out, out),
                4 + 2 * len(xs),
                4 * size * width * hidden,
                4 * hidden * width + 4 * size * width,
                [pltpu.VMEM((size, width), BF16), pltpu.VMEM((size, hidden), BF16)],
            )(after(info, *others), *xs, *ys, gates, up_weight, down_weight)

        def total(stay, given, more=None):
            t = stay.astype(F32) + given.astype(F32)
            return t if more is None else t + more.astype(F32)

        done = {}
        pairs = [(latent, latent)]
        for d in range(1, far + 1):
            below, above = pairs[-1]
            beside = []
            if d == 1:
                swapped = swap(latent)
                beside = [*out_blocks, swapped]
                hand(latent)
            elif d == 2:
                beside = [*pack(below), *handed]
                hand()
            elif d == 3:
                done[1] = expert(pairs[1], [(1, 0), (2, 0)], below)
                beside = [*done[1], *handed]
            if d == far:
                done[d - 1] = expert(pairs[d - 1], [(2 * d - 3, 0), (2 * d - 2, 0)])
                beside = [*done[d - 1]]
                below, above = below[:half_rows], above[half_rows:]
            pairs.append(step(below, above, *beside))
        below, above = pairs[far]
        done[far] = expert([below, above], [(wide - 1, 0), (wide - 1, half_rows)])

        given = swap(done[far][1])
        back = total(done[far][0], given).astype(BF16)
        out_step(*pairs[far])
        back = after(back, *out_blocks)
        done[far - 2] = expert(
            pairs[far - 2], [(2 * far - 5, 0), (2 * far - 4, 0)], back
        )
        beside = [*done[far - 2]]
        out_step(back)
        to_above, to_below = step(
            back[:half_rows], back[half_rows:], *beside, *out_blocks
        )
        for d in range(far - 1, 0, -1):
            given = swap(done[d][1])
            below = total(done[d][0][:rows], given[:rows])
            above = total(done[d][0][rows:], given[rows:])
            if d == far - 1:
                above = jnp.concatenate(
                    [above[:half_rows] + to_above.astype(F32), above[half_rows:]], axis=0
                )
                below = jnp.concatenate(
                    [below[:half_rows], below[half_rows:] + to_below.astype(F32)], axis=0
                )
            else:
                above, below = above + to_above.astype(F32), below + to_below.astype(F32)
            above, below = above.astype(BF16), below.astype(BF16)
            beside = []
            if d > 1 and d - 1 not in done:
                done[d - 1] = expert(
                    pairs[d - 1], [(2 * d - 3, 0), (2 * d - 2, 0)], to_above, to_below
                )
                beside += done[d - 1]
            if d == 2:
                done[0] = expert(
                    [latent], [(0, 0)], to_above, to_below, swapped=[swapped]
                )
                beside += done[0]
            if d == 1:
                given0 = swap(done[0][1])
                beside += [given0]
            if len(out_blocks) < 2 * far:
                out_step(to_above, to_below)
                beside += out_blocks
            while len(packs) < len(out_blocks) // 2:
                beside += pack(to_above)
            beside += handed[2:]
            if len(handed) < far:
                hand(to_above)
            if d == 1:
                full = kernel_call(
                    functools.partial(assemble_body, out_depth),
                    shape(width, columns),
                    1,
                    width * columns,
                    4 * width * columns,
                    [pltpu.SemaphoreType.DMA((1 + 2 * len(out_blocks),))],
                    1 + len(out_blocks) + len(handed),
                )(side_info, w_out, *out_blocks, *handed)
                beside = [*beside[: -len(handed)], full]
            to_above, to_below = step(above, below, *beside)
        mixture = total(done[0][0], given0, to_above)
        mixture = (mixture + to_below.astype(F32)).astype(BF16)
        return kernel_call(
            final_body,
            shape(rows, columns),
            5,
            2 * rows * width * columns,
            2 * width * columns + 4 * rows * columns,
            [pltpu.VMEM((rows, width), BF16)],
        )(info, kept, mixture, swap(mixture), full)

    return local


def solution(mesh):
    in_specs = (
        P(("groups", "wide"), None),
        P(),
        P("wide", None),
        P("wide", "narrow"),
        P("wide", None, "narrow"),
        P("wide", "narrow", None),
        P(("groups", "wide"), None),
        P(("groups", "wide"), None),
    )
    out_specs = P(("groups", "wide"), "narrow")
    local = make_local(ring_order(mesh))
    return jax.shard_map(
        local, mesh=mesh, in_specs=in_specs, out_specs=out_specs, check_vma=False
    )
```

```python
import functools

import jax
import jax.numpy as jnp
from jax import lax
from jax.experimental import pallas as pl
from jax.experimental.pallas import tpu as pltpu
from jax.sharding import PartitionSpec as P

F32, BF16 = jnp.float32, jnp.bfloat16
VMEM = pl.BlockSpec(memory_space=pltpu.VMEM)
SMEM = pl.BlockSpec(memory_space=pltpu.SMEM)
ANY = pl.BlockSpec(memory_space=pl.ANY)
LIMIT, BIG = 20 * 2**20, 20 * 2**20


def kernel_call(body, out, n_in, flops, nbytes, scratch=(), n_any=0, limit=LIMIT):
    return pl.pallas_call(
        body,
        out_shape=out,
        in_specs=[SMEM] + [VMEM] * (n_in - 1) + [ANY] * n_any,
        out_specs=jax.tree.map(lambda _: VMEM, out),
        scratch_shapes=list(scratch),
        compiler_params=pltpu.CompilerParams(vmem_limit_bytes=limit),
        cost_estimate=pl.CostEstimate(
            flops=flops, bytes_accessed=nbytes, transcendentals=0
        ),
    )


def norm_body(info, tokens, gain, out):
    rows, model = tokens.shape
    step = 16

    @pl.loop(0, rows // step)
    def _(i):
        at = pl.ds(pl.multiple_of(i * step, step), step)
        x = tokens[at, :].astype(F32)
        mean = jnp.sum(x * x, axis=1, keepdims=True) * (1.0 / model)
        x = tokens[at, :].astype(F32) * lax.rsqrt(mean + 1e-05) * gain[...]
        out[at, :] = x.astype(BF16)


def fetch(sources, places, done):
    copies = [
        pltpu.make_async_copy(a, b, done.at[i])
        for i, (a, b) in enumerate(zip(sources, places))
    ]
    for copy in copies:
        copy.start()

    def arrived(i):
        copies[i].wait()
        return places[i]

    return arrived


def places_for(arrays):
    return [pltpu.VMEM(a.shape, a.dtype) for a in arrays] + [
        pltpu.SemaphoreType.DMA((len(arrays),))
    ]


def start_body(wide, info, ids, weights, tokens, w_in, raw, block, done):
    rows, depth, quarter = raw.shape[0], w_in.shape[0], block.shape[1]
    columns = pl.ds(pl.multiple_of(info[1] * quarter, quarter), quarter)
    parts = done.shape[0] // 2
    copies = []
    for i in range(parts):
        size = rows // parts
        at = pl.ds(pl.multiple_of(info[0] * rows + i * size, size), size)
        to = raw.at[pl.ds(i * size, size), :]
        copies.append(pltpu.make_async_copy(tokens.at[at, :], to, done.at[i]))
        at = pl.ds(i * (depth // parts), depth // parts)
        copies.append(
            pltpu.make_async_copy(w_in.at[at, columns], block.at[at, :], done.at[parts + i])
        )
    for copy in copies:
        copy.start()
    number = lax.broadcasted_iota(jnp.int32, (wide, ids.shape[1]), 0)
    dense = jnp.zeros(number.shape, F32)
    for k in range(ids.shape[0]):
        dense += jnp.where(ids[k : k + 1, :] == number, weights[k : k + 1, :], 0.0)
    terms = []
    for _ in range(3):
        terms.append(dense.astype(BF16).astype(F32))
        dense = dense - terms[-1]
    empty = block.shape[0] - depth - 3 * wide
    if empty:
        terms.append(jnp.zeros((empty, ids.shape[1]), F32))
    block[depth:, :] = jnp.concatenate(terms, axis=0).astype(BF16)
    for copy in copies:
        copy.wait()


def pack_body(info, first, second, out, done):
    size = first.shape[0]
    places = [out.at[pl.ds(0, size), :], out.at[pl.ds(size, second.shape[0]), :]]
    arrived = fetch([first, second], places, done)
    arrived(0), arrived(1)


def near_body(depth, n, info, *refs):
    lefts, rest = refs[:n], refs[n:]
    count = (len(rest) - 3) // 2
    blocks, out, columns = rest[:count], rest[count], rest[count + 1]
    places, done = rest[count + 2 : -1], rest[-1]
    arrived = fetch(blocks, places, done)
    total = None
    for i in range(count):
        at = pl.ds(pl.multiple_of(info[2 + i] * depth, depth), depth)
        left = jnp.concatenate([a[:, at] for a in lefts], axis=0)
        term = jnp.dot(left, arrived(i)[:depth, :], preferred_element_type=F32)
        total = term if total is None else total + term
    out[...] = total
    at = pl.ds(pl.multiple_of(info[2 + count] * depth, depth), depth)
    columns[...] = jnp.concatenate([a[:, at] for a in lefts], axis=0)


def far_body(depth, info, partial, left, low, high, out):
    right = jnp.concatenate([low[: depth // 2, :], high[: depth // 2, :]], axis=0)
    total = jnp.dot(left[...], right, preferred_element_type=F32) + partial[...]
    total = total.astype(BF16)
    core, half = info[0], total.shape[0] // 2
    out[pl.ds(pl.multiple_of(core * half, half), half), :] = total[:half]
    out[pl.ds(pl.multiple_of((1 - core) * half, half), half), :] = total[half:]


def mine_body(depth, wide, first, info, normed, *refs):
    refs, (out, gates) = list(refs[:-2]), refs[-2:]
    total = lines = None
    if first:
        total, lines = refs.pop()[...], refs.pop()[...]
    other = refs.pop() if first == wide - 1 else None
    extra = -(-3 * wide // 16) * 16
    number = lax.broadcasted_iota(jnp.int32, (extra, refs[0].shape[1]), 0)
    chosen = (number % wide == info[1]) & (number < 3 * wide)
    i = first
    while refs:
        block = refs.pop(0)
        if i < wide - 1:
            right, carried = block[:depth, :], block[depth:, :]
        else:
            high = refs.pop(0)
            right = [block[...], high[: depth // 2, :]]
            right, carried = jnp.concatenate(right, axis=0), high[depth // 2 :, :]
        at = pl.ds(pl.multiple_of(info[2 + i] * depth, depth), depth)
        term = jnp.dot(normed[:, at], right, preferred_element_type=F32)
        total = term if total is None else total + term
        line = jnp.where(chosen, carried.astype(F32), 0.0)
        line = jnp.sum(line, axis=0, keepdims=True)
        lines = line if lines is None else jnp.concatenate([lines, line], axis=0)
        i += 1
    if other is None:
        out[...] = total
        gates[...] = lines
        return
    size = total.shape[1]
    side = info[2 + wide]
    out[:, pl.ds(pl.multiple_of(side * size, size), size)] = total.astype(BF16)
    out[:, pl.ds(pl.multiple_of((1 - side) * size, size), size)] = other[...]
    gates[...] = lines.T


def expert_body(columns, info, *refs):
    n = len(columns)
    own, other = refs[:n], refs[n : 2 * n]
    gates, up, down, stay, give, x, hid = refs[2 * n :]
    core = info[0]
    half = own[0].shape[1]
    here = pl.ds(pl.multiple_of(core * half, half), half)
    there = pl.ds(pl.multiple_of((1 - core) * half, half), half)
    begin = 0
    for a, b in zip(own, other):
        size = a.shape[0]
        x[begin : begin + size, here] = a[...]
        x[begin : begin + size, there] = b[...]
        begin += size
    hidden = up.shape[0]
    chunk = hidden if hidden % 128 else max(c for c in range(128, 513, 128) if hidden % c == 0)
    for i in range(hidden // chunk):
        at = slice(i * chunk, (i + 1) * chunk)
        h = lax.dot_general(
            x[...], up[at, :], (((1,), (1,)), ((), ())), preferred_element_type=F32
        )
        hid[:, at] = jnp.square(jnp.maximum(h, 0.0)).astype(BF16)
    for columns_at, out in ((here, stay), (there, give)):
        total = jnp.dot(hid[...], down[:, columns_at], preferred_element_type=F32)
        begin = 0
        for j, (column, first) in enumerate(columns):
            size = own[j].shape[0]
            gate = gates[first : first + size, column : column + 1]
            rows = slice(begin, begin + size)
            out[rows, :] = (total[rows] * gate).astype(BF16)
            begin += size


def assemble_body(depth, info, *rest):
    *blocks, full, done = rest
    side, me = info[1], info[2]
    count = (len(blocks) - 1) * 2 // 3
    pairs = [(b, b.shape[0] // 2) for b in blocks[1 + count :]]
    blocks = blocks[: 1 + count] + [
        b.at[pl.ds(i * size, size), :] for b, size in pairs for i in range(2)
    ]
    span = blocks[1].shape[1]
    places = [full.at[pl.ds(pl.multiple_of(me * depth, depth), depth), :]]
    for number in range(2):
        at = pl.ds(pl.multiple_of((side + number) % 2 * span, span), span)
        for i in range(count):
            size = blocks[1 + i].shape[0]
            begin = info[2 + min(1 + i, count - 1)] * depth
            if i == count - 1:
                begin = begin + size
            places.append(full.at[pl.ds(pl.multiple_of(begin, size), size), at])
    arrived = fetch(blocks, places, done)
    for i in range(len(blocks)):
        arrived(i)


def half_body(info, kept, mine, full, out):
    half, step = mine.shape[1], 512
    rows = pl.ds(pl.multiple_of(info[0] * half, half), half)
    for i in range(full.shape[1] // step):
        at = slice(i * step, (i + 1) * step)
        branch = jnp.dot(mine[...], full[rows, at], preferred_element_type=F32)
        out[:, at] = kept[:, at].astype(F32) + branch


def final_body(info, partial, back, full, out, ready, done):
    half, step, copies = back.shape[1], 512, []
    rows = pl.ds(pl.multiple_of((1 - info[0]) * half, half), half)
    for i in range(full.shape[1] // step):
        at = slice(i * step, (i + 1) * step)
        branch = jnp.dot(back[...], full[rows, at], preferred_element_type=F32)
        ready[:, at] = (partial[:, at] + branch).astype(BF16)
        copies.append(pltpu.make_async_copy(ready.at[:, at], out.at[:, at], done.at[i]))
        copies[-1].start()
    for copy in copies:
        copy.wait()


def after(x, *others):
    return lax.optimization_barrier((x, others))[0]


def both(*xs):
    return lax.optimization_barrier(xs)


def ring_order(mesh):
    wide = mesh.shape["wide"]
    line = mesh.devices.reshape(-1, wide, mesh.shape["narrow"])[0, :, 0]
    places = [tuple(getattr(d, "coords", (0,))) for d in line]
    spread = [len(set(c)) for c in zip(*places)]
    if sum(s > 1 for s in spread) == 2 and wide % 2 == 0:
        return list(range(0, wide, 2)) + list(range(wide - 1, 0, -2))
    return list(range(wide))


def make_local(order):
    wide = len(order)
    far = wide // 2
    up_perm = [(order[i], order[(i + 1) % wide]) for i in range(wide)]
    down_perm = [(order[(i + 1) % wide], order[i]) for i in range(wide)]
    offsets = [0] + [s * d for d in range(1, far) for s in (-1, 1)] + [far]
    sources = [[order[(order.index(i) + o) % wide] for o in offsets] for i in range(wide)]

    def local(tokens, norm_gain, w_in, w_out, w_up, w_down, expert_ids, gate_weights):
        groups = lax.axis_size("groups")
        side = lax.axis_index("groups") % 2
        me = lax.axis_index("wide")
        core = lax.axis_index("narrow")
        rows, model = tokens.shape
        half_rows = rows // 2
        depth, width = w_in.shape
        half, quarter = width // 2, width // 4
        info = jnp.concatenate(
            [
                jnp.stack([core, me]),
                jnp.asarray(sources, jnp.int32)[me],
                side.reshape(1),
            ]
        ).astype(jnp.int32)

        def up(x):
            return lax.ppermute(x, "wide", up_perm)

        def down(x):
            return lax.ppermute(x, "wide", down_perm)

        def swap(x):
            return lax.ppermute(x, "narrow", [(0, 1), (1, 0)])

        def across(x):
            return lax.ppermute(x, "groups", [(i, i ^ 1) for i in range(groups)])

        def shape(*dims, kind=BF16):
            return jax.ShapeDtypeStruct(dims, kind)

        columns = w_out.shape[1]
        out_half = lax.dynamic_slice_in_dim(
            w_out, side * (columns // 2), columns // 2, 1
        )
        out_depth = w_out.shape[0]
        out_blocks = []
        out_below = out_above = out_half

        def out_step(*others, beside=()):
            nonlocal out_below, out_above
            out_below, out_above = after((out_below, out_above), *others)
            if len(out_blocks) == 2 * far - 2:
                cut = out_depth // 2
                out_below, out_above = out_below[:cut], out_above[cut:]
            moved = both(up(out_below), down(out_above), *beside)
            out_below, out_above = moved[:2]
            out_blocks.extend([out_below, out_above])

        handed = []

        packs = []

        def pack(*others):
            pair = out_blocks[2 * len(packs) :][:2]
            out = shape(2 * pair[0].shape[0], pair[0].shape[1])
            one = kernel_call(
                pack_body,
                out,
                1,
                out.size,
                4 * out.size,
                [pltpu.SemaphoreType.DMA((2,))],
                2,
            )(after(info, *others), *pair)
            packs.append(one)
            return [one]

        def hand(*others):
            handed.append(across(after(packs[len(handed)], *others)))

        out_step()

        extra = -(-3 * wide // 16) * 16
        raw, block = pl.pallas_call(
            functools.partial(start_body, wide),
            out_shape=(shape(half_rows, model), shape(depth + extra, quarter)),
            in_specs=[SMEM, VMEM, VMEM, ANY, ANY],
            out_specs=(VMEM, VMEM),
            scratch_shapes=[pltpu.SemaphoreType.DMA((8,))],
        )(
            jnp.stack([core, core * 2 + side]).astype(jnp.int32),
            expert_ids.T,
            gate_weights.T,
            tokens,
            w_in,
        )

        def norm(x, *others):
            return kernel_call(
                norm_body,
                shape(*x.shape),
                3,
                8 * x.size,
                4 * x.size,
            )(after(info, *others), x, norm_gain.reshape(1, model))

        def step(below, above, *beside):
            return both(up(below), down(above), *beside)[:2]

        first = across(raw)
        flops = 2 * rows * model * quarter
        nbytes = 2 * (rows * model + model * quarter)

        def near(*lefts):
            return kernel_call(
                functools.partial(near_body, depth, len(lefts)),
                (shape(rows, quarter, kind=F32), shape(rows, depth)),
                1 + len(lefts),
                flops,
                nbytes,
                places_for(blocks),
                len(blocks),
                BIG,
            )(info, *lefts, *blocks)

        def mine(first, part, *before, others=()):
            last = first + len(part) > wide
            outs = shape(rows, half) if last else shape(rows, quarter, kind=F32)
            number = min(first + len(part), wide)
            lines = shape(rows, wide, kind=F32) if last else shape(number, rows, kind=F32)
            return kernel_call(
                functools.partial(mine_body, depth, wide, first),
                (outs, lines),
                2 + len(part) + len(before),
                flops * len(part) // wide,
                nbytes * len(part) // wide,
            )(after(info, *others), normed, *part, *before)

        blocks = [block]
        below = above = block
        lat_mine = []
        for d in range(1, far):
            beside = []
            if d == 1:
                normed = norm(tokens, block)
                beside = [normed]
            else:
                begin = 0 if d == 2 else 2 * d - 3
                lat_mine = mine(begin, blocks[begin:], *lat_mine[::-1])
                beside = [*lat_mine]
            if d == 2:
                kept = lax.dynamic_slice_in_dim(
                    after(tokens, below), core * columns, columns, 1
                )
                beside += [kept, *pack(below)]
            elif d == 3:
                first = norm(first, below)
                beside += [first]
            below, above = step(below, above, *beside)
            blocks += [below, above]
        second = swap(after(first, below))
        near_there = near(first, second)
        begin = len(blocks) - 2
        lat_mine = mine(begin, blocks[begin:], *lat_mine[::-1])
        ends = step(below[: depth // 2], above[depth // 2 :], *near_there, *lat_mine)

        lat_there = kernel_call(
            functools.partial(far_body, depth),
            shape(rows, quarter),
            5,
            flops // wide,
            nbytes // wide,
        )(info, *near_there, *ends)
        lat_other = across(lat_there)
        out_step(lat_there)
        latent, gates = mine(len(blocks), ends, lat_other, *lat_mine[::-1])
        side_info = info.at[1].set(side.astype(jnp.int32))
        up_weight, down_weight = w_up[0].T, w_down[0]
        hidden = up_weight.shape[0]

        def expert(xs, columns, *others, swapped=None):
            size = sum(x.shape[0] for x in xs)
            out = shape(size, half)
            ys = swapped or [swap(x) for x in xs]
            return kernel_call(
                functools.partial(expert_body, columns),
                (out, out),
                4 + 2 * len(xs),
                4 * size * width * hidden,
                4 * hidden * width + 4 * size * width,
                [pltpu.VMEM((size, width), BF16), pltpu.VMEM((size, hidden), BF16)],
            )(after(info, *others), *xs, *ys, gates, up_weight, down_weight)

        def total(stay, given, more=None):
            t = stay.astype(F32) + given.astype(F32)
            return t if more is None else t + more.astype(F32)

        done = {}
        pairs = [(latent, latent)]
        for d in range(1, far + 1):
            below, above = pairs[-1]
            beside = []
            if d == 1:
                swapped = swap(latent)
                beside = [*out_blocks, swapped]
                hand(latent)
            elif d == 2:
                beside = [*pack(below), *handed]
                hand()
            elif d == 3:
                done[1] = expert(pairs[1], [(1, 0), (2, 0)], below)
                beside = [*done[1], *handed]
            if d == far:
                done[d - 1] = expert(pairs[d - 1], [(2 * d - 3, 0), (2 * d - 2, 0)])
                beside = [*done[d - 1]]
                below, above = below[:half_rows], above[half_rows:]
            pairs.append(step(below, above, *beside))
        below, above = pairs[far]
        done[far] = expert([below, above], [(wide - 1, 0), (wide - 1, half_rows)])

        given = swap(done[far][1])
        back = total(done[far][0], given).astype(BF16)
        out_step(*pairs[far])
        back = after(back, *out_blocks)
        done[far - 2] = expert(
            pairs[far - 2], [(2 * far - 5, 0), (2 * far - 4, 0)], back
        )
        beside = [*done[far - 2]]
        out_step(back)
        to_above, to_below = step(
            back[:half_rows], back[half_rows:], *beside, *out_blocks
        )
        for d in range(far - 1, 0, -1):
            given = swap(done[d][1])
            below = total(done[d][0][:rows], given[:rows])
            above = total(done[d][0][rows:], given[rows:])
            if d == far - 1:
                above = jnp.concatenate(
                    [above[:half_rows] + to_above.astype(F32), above[half_rows:]], axis=0
                )
                below = jnp.concatenate(
                    [below[:half_rows], below[half_rows:] + to_below.astype(F32)], axis=0
                )
            else:
                above, below = above + to_above.astype(F32), below + to_below.astype(F32)
            above, below = above.astype(BF16), below.astype(BF16)
            beside = []
            if d > 1 and d - 1 not in done:
                done[d - 1] = expert(
                    pairs[d - 1], [(2 * d - 3, 0), (2 * d - 2, 0)], to_above, to_below
                )
                beside += done[d - 1]
            if d == 2:
                done[0] = expert(
                    [latent], [(0, 0)], to_above, to_below, swapped=[swapped]
                )
                beside += done[0]
            if d == 1:
                given0 = swap(done[0][1])
                beside += [given0]
            if len(out_blocks) < 2 * far:
                out_step(to_above, to_below)
                beside += out_blocks
            while len(packs) < len(out_blocks) // 2:
                beside += pack(to_above)
            beside += handed[2:]
            if len(handed) < far:
                hand(to_above)
            if d == 1:
                full = kernel_call(
                    functools.partial(assemble_body, out_depth),
                    shape(width, columns),
                    1,
                    width * columns,
                    4 * width * columns,
                    [pltpu.SemaphoreType.DMA((1 + 2 * len(out_blocks),))],
                    1 + len(out_blocks) + len(handed),
                )(side_info, w_out, *out_blocks, *handed)
                beside = [*beside[: -len(handed)], full]
            to_above, to_below = step(above, below, *beside)
        mixture = total(done[0][0], given0, to_above)
        mixture = (mixture + to_below.astype(F32)).astype(BF16)
        partial = kernel_call(
            half_body,
            shape(rows, columns, kind=F32),
            4,
            rows * width * columns,
            width * columns + 6 * rows * columns,
        )(info, kept, mixture, full)
        back, partial = both(swap(mixture), partial)
        return pl.pallas_call(
            final_body,
            out_shape=shape(rows, columns),
            in_specs=[SMEM] + [VMEM] * 3,
            out_specs=ANY,
            scratch_shapes=[
                pltpu.VMEM((rows, columns), BF16),
                pltpu.SemaphoreType.DMA((columns // 512,)),
            ],
            compiler_params=pltpu.CompilerParams(vmem_limit_bytes=LIMIT),
        )(info, partial, back, full)

    return local


def solution(mesh):
    in_specs = (
        P(("groups", "wide"), None),
        P(),
        P("wide", None),
        P("wide", "narrow"),
        P("wide", None, "narrow"),
        P("wide", "narrow", None),
        P(("groups", "wide"), None),
        P(("groups", "wide"), None),
    )
    out_specs = P(("groups", "wide"), "narrow")
    local = make_local(ring_order(mesh))
    return jax.shard_map(
        local, mesh=mesh, in_specs=in_specs, out_specs=out_specs, check_vma=False
    )
```

```python
import functools

import jax
import jax.numpy as jnp
from jax import lax
from jax.experimental import pallas as pl
from jax.experimental.pallas import tpu as pltpu
from jax.sharding import PartitionSpec as P

F32, BF16 = jnp.float32, jnp.bfloat16
VMEM = pl.BlockSpec(memory_space=pltpu.VMEM)
SMEM = pl.BlockSpec(memory_space=pltpu.SMEM)
ANY = pl.BlockSpec(memory_space=pl.ANY)
LIMIT, BIG = 20 * 2**20, 20 * 2**20


def kernel_call(body, out, n_in, flops, nbytes, scratch=(), n_any=0, limit=LIMIT):
    return pl.pallas_call(
        body,
        out_shape=out,
        in_specs=[SMEM] + [VMEM] * (n_in - 1) + [ANY] * n_any,
        out_specs=jax.tree.map(lambda _: VMEM, out),
        scratch_shapes=list(scratch),
        compiler_params=pltpu.CompilerParams(vmem_limit_bytes=limit),
        cost_estimate=pl.CostEstimate(
            flops=flops, bytes_accessed=nbytes, transcendentals=0
        ),
    )


def norm_body(info, tokens, gain, out):
    rows, model = tokens.shape
    step = 32

    @pl.loop(0, rows // step)
    def _(i):
        at = pl.ds(pl.multiple_of(i * step, step), step)
        x = tokens[at, :].astype(F32)
        mean = jnp.sum(x * x, axis=1, keepdims=True) * (1.0 / model)
        x = tokens[at, :].astype(F32) * lax.rsqrt(mean + 1e-05) * gain[...]
        out[at, :] = x.astype(BF16)


def fetch(sources, places, done):
    copies = [
        pltpu.make_async_copy(a, b, done.at[i])
        for i, (a, b) in enumerate(zip(sources, places))
    ]
    for copy in copies:
        copy.start()

    def arrived(i):
        copies[i].wait()
        return places[i]

    return arrived


def places_for(arrays):
    return [pltpu.VMEM(a.shape, a.dtype) for a in arrays] + [
        pltpu.SemaphoreType.DMA((len(arrays),))
    ]


def start_body(wide, info, ids, weights, tokens, w_in, raw, block, done):
    rows, depth, quarter = raw.shape[0], w_in.shape[0], block.shape[1]
    columns = pl.ds(pl.multiple_of(info[1] * quarter, quarter), quarter)
    parts = done.shape[0] // 2
    copies = []
    for i in range(parts):
        size = rows // parts
        at = pl.ds(pl.multiple_of(info[0] * rows + i * size, size), size)
        to = raw.at[pl.ds(i * size, size), :]
        copies.append(pltpu.make_async_copy(tokens.at[at, :], to, done.at[i]))
        at = pl.ds(i * (depth // parts), depth // parts)
        copies.append(
            pltpu.make_async_copy(w_in.at[at, columns], block.at[at, :], done.at[parts + i])
        )
    for copy in copies:
        copy.start()
    number = lax.broadcasted_iota(jnp.int32, (wide, ids.shape[1]), 0)
    dense = jnp.zeros(number.shape, F32)
    for k in range(ids.shape[0]):
        dense += jnp.where(ids[k : k + 1, :] == number, weights[k : k + 1, :], 0.0)
    terms = []
    for _ in range(3):
        terms.append(dense.astype(BF16).astype(F32))
        dense = dense - terms[-1]
    empty = block.shape[0] - depth - 3 * wide
    if empty:
        terms.append(jnp.zeros((empty, ids.shape[1]), F32))
    block[depth:, :] = jnp.concatenate(terms, axis=0).astype(BF16)
    for copy in copies:
        copy.wait()


def pack_body(info, first, second, out, done):
    size = first.shape[0]
    places = [out.at[pl.ds(0, size), :], out.at[pl.ds(size, second.shape[0]), :]]
    arrived = fetch([first, second], places, done)
    arrived(0), arrived(1)


def near_body(depth, n, info, *refs):
    lefts, rest = refs[:n], refs[n:]
    count = (len(rest) - 3) // 2
    blocks, out, columns = rest[:count], rest[count], rest[count + 1]
    places, done = rest[count + 2 : -1], rest[-1]
    arrived = fetch(blocks, places, done)
    total = None
    for i in range(count):
        at = pl.ds(pl.multiple_of(info[2 + i] * depth, depth), depth)
        left = jnp.concatenate([a[:, at] for a in lefts], axis=0)
        term = jnp.dot(left, arrived(i)[:depth, :], preferred_element_type=F32)
        total = term if total is None else total + term
    out[...] = total
    at = pl.ds(pl.multiple_of(info[2 + count] * depth, depth), depth)
    columns[...] = jnp.concatenate([a[:, at] for a in lefts], axis=0)


def far_body(depth, info, partial, left, low, high, out):
    right = jnp.concatenate([low[: depth // 2, :], high[: depth // 2, :]], axis=0)
    total = jnp.dot(left[...], right, preferred_element_type=F32) + partial[...]
    total = total.astype(BF16)
    core, half = info[0], total.shape[0] // 2
    out[pl.ds(pl.multiple_of(core * half, half), half), :] = total[:half]
    out[pl.ds(pl.multiple_of((1 - core) * half, half), half), :] = total[half:]


def mine_body(depth, wide, first, info, normed, *refs):
    refs, (out, gates) = list(refs[:-2]), refs[-2:]
    total = lines = None
    if first:
        total, lines = refs.pop()[...], refs.pop()[...]
    other = refs.pop() if first == wide - 1 else None
    extra = -(-3 * wide // 16) * 16
    number = lax.broadcasted_iota(jnp.int32, (extra, refs[0].shape[1]), 0)
    chosen = (number % wide == info[1]) & (number < 3 * wide)
    i = first
    while refs:
        block = refs.pop(0)
        if i < wide - 1:
            right, carried = block[:depth, :], block[depth:, :]
        else:
            high = refs.pop(0)
            right = [block[...], high[: depth // 2, :]]
            right, carried = jnp.concatenate(right, axis=0), high[depth // 2 :, :]
        at = pl.ds(pl.multiple_of(info[2 + i] * depth, depth), depth)
        term = jnp.dot(normed[:, at], right, preferred_element_type=F32)
        total = term if total is None else total + term
        line = jnp.where(chosen, carried.astype(F32), 0.0)
        line = jnp.sum(line, axis=0, keepdims=True)
        lines = line if lines is None else jnp.concatenate([lines, line], axis=0)
        i += 1
    if other is None:
        out[...] = total
        gates[...] = lines
        return
    size = total.shape[1]
    side = info[2 + wide]
    out[:, pl.ds(pl.multiple_of(side * size, size), size)] = total.astype(BF16)
    out[:, pl.ds(pl.multiple_of((1 - side) * size, size), size)] = other[...]
    gates[...] = lines.T


def expert_body(columns, info, *refs):
    n = len(columns)
    own, other = refs[:n], refs[n : 2 * n]
    gates, up, down, stay, give, x, hid = refs[2 * n :]
    core = info[0]
    half = own[0].shape[1]
    here = pl.ds(pl.multiple_of(core * half, half), half)
    there = pl.ds(pl.multiple_of((1 - core) * half, half), half)
    begin = 0
    for a, b in zip(own, other):
        size = a.shape[0]
        x[begin : begin + size, here] = a[...]
        x[begin : begin + size, there] = b[...]
        begin += size
    hidden = up.shape[0]
    chunk = hidden if hidden % 128 else max(c for c in range(128, 513, 128) if hidden % c == 0)
    for i in range(hidden // chunk):
        at = slice(i * chunk, (i + 1) * chunk)
        h = lax.dot_general(
            x[...], up[at, :], (((1,), (1,)), ((), ())), preferred_element_type=F32
        )
        hid[:, at] = jnp.square(jnp.maximum(h, 0.0)).astype(BF16)
    for columns_at, out in ((here, stay), (there, give)):
        total = jnp.dot(hid[...], down[:, columns_at], preferred_element_type=F32)
        begin = 0
        for j, (column, first) in enumerate(columns):
            size = own[j].shape[0]
            gate = gates[first : first + size, column : column + 1]
            rows = slice(begin, begin + size)
            out[rows, :] = (total[rows] * gate).astype(BF16)
            begin += size


def assemble_body(depth, info, *rest):
    *blocks, full, done = rest
    side, me = info[1], info[2]
    count = (len(blocks) - 1) * 2 // 3
    pairs = [(b, b.shape[0] // 2) for b in blocks[1 + count :]]
    blocks = blocks[: 1 + count] + [
        b.at[pl.ds(i * size, size), :] for b, size in pairs for i in range(2)
    ]
    span = blocks[1].shape[1]
    places = [full.at[pl.ds(pl.multiple_of(me * depth, depth), depth), :]]
    for number in range(2):
        at = pl.ds(pl.multiple_of((side + number) % 2 * span, span), span)
        for i in range(count):
            size = blocks[1 + i].shape[0]
            begin = info[2 + min(1 + i, count - 1)] * depth
            if i == count - 1:
                begin = begin + size
            places.append(full.at[pl.ds(pl.multiple_of(begin, size), size), at])
    arrived = fetch(blocks, places, done)
    for i in range(len(blocks)):
        arrived(i)


def half_body(info, kept, mine, full, out):
    half, step = mine.shape[1], 512
    rows = pl.ds(pl.multiple_of(info[0] * half, half), half)
    for i in range(full.shape[1] // step):
        at = slice(i * step, (i + 1) * step)
        branch = jnp.dot(mine[...], full[rows, at], preferred_element_type=F32)
        out[:, at] = kept[:, at].astype(F32) + branch


def final_body(info, partial, back, full, out, ready, done):
    half, step, copies = back.shape[1], 512, []
    rows = pl.ds(pl.multiple_of((1 - info[0]) * half, half), half)
    for i in range(full.shape[1] // step):
        at = slice(i * step, (i + 1) * step)
        branch = jnp.dot(back[...], full[rows, at], preferred_element_type=F32)
        ready[:, at] = (partial[:, at] + branch).astype(BF16)
        copies.append(pltpu.make_async_copy(ready.at[:, at], out.at[:, at], done.at[i]))
        copies[-1].start()
    for copy in copies:
        copy.wait()


def after(x, *others):
    return lax.optimization_barrier((x, others))[0]


def both(*xs):
    return lax.optimization_barrier(xs)


def ring_order(mesh):
    wide = mesh.shape["wide"]
    line = mesh.devices.reshape(-1, wide, mesh.shape["narrow"])[0, :, 0]
    places = [tuple(getattr(d, "coords", (0,))) for d in line]
    spread = [len(set(c)) for c in zip(*places)]
    if sum(s > 1 for s in spread) == 2 and wide % 2 == 0:
        return list(range(0, wide, 2)) + list(range(wide - 1, 0, -2))
    return list(range(wide))


def make_local(order):
    wide = len(order)
    far = wide // 2
    up_perm = [(order[i], order[(i + 1) % wide]) for i in range(wide)]
    down_perm = [(order[(i + 1) % wide], order[i]) for i in range(wide)]
    offsets = [0] + [s * d for d in range(1, far) for s in (-1, 1)] + [far]
    sources = [[order[(order.index(i) + o) % wide] for o in offsets] for i in range(wide)]

    def local(tokens, norm_gain, w_in, w_out, w_up, w_down, expert_ids, gate_weights):
        groups = lax.axis_size("groups")
        side = lax.axis_index("groups") % 2
        me = lax.axis_index("wide")
        core = lax.axis_index("narrow")
        rows, model = tokens.shape
        half_rows = rows // 2
        depth, width = w_in.shape
        half, quarter = width // 2, width // 4
        info = jnp.concatenate(
            [
                jnp.stack([core, me]),
                jnp.asarray(sources, jnp.int32)[me],
                side.reshape(1),
            ]
        ).astype(jnp.int32)

        def up(x):
            return lax.ppermute(x, "wide", up_perm)

        def down(x):
            return lax.ppermute(x, "wide", down_perm)

        def swap(x):
            return lax.ppermute(x, "narrow", [(0, 1), (1, 0)])

        def across(x):
            return lax.ppermute(x, "groups", [(i, i ^ 1) for i in range(groups)])

        def shape(*dims, kind=BF16):
            return jax.ShapeDtypeStruct(dims, kind)

        columns = w_out.shape[1]
        out_half = lax.dynamic_slice_in_dim(
            w_out, side * (columns // 2), columns // 2, 1
        )
        out_depth = w_out.shape[0]
        out_blocks = []
        out_below = out_above = out_half

        def out_step(*others, beside=()):
            nonlocal out_below, out_above
            out_below, out_above = after((out_below, out_above), *others)
            if len(out_blocks) == 2 * far - 2:
                cut = out_depth // 2
                out_below, out_above = out_below[:cut], out_above[cut:]
            moved = both(up(out_below), down(out_above), *beside)
            out_below, out_above = moved[:2]
            out_blocks.extend([out_below, out_above])

        handed = []

        packs = []

        def pack(*others):
            pair = out_blocks[2 * len(packs) :][:2]
            out = shape(2 * pair[0].shape[0], pair[0].shape[1])
            one = kernel_call(
                pack_body,
                out,
                1,
                out.size,
                4 * out.size,
                [pltpu.SemaphoreType.DMA((2,))],
                2,
            )(after(info, *others), *pair)
            packs.append(one)
            return [one]

        def hand(*others):
            handed.append(across(after(packs[len(handed)], *others)))

        out_step()

        extra = -(-3 * wide // 16) * 16
        raw, block = pl.pallas_call(
            functools.partial(start_body, wide),
            out_shape=(shape(half_rows, model), shape(depth + extra, quarter)),
            in_specs=[SMEM, VMEM, VMEM, ANY, ANY],
            out_specs=(VMEM, VMEM),
            scratch_shapes=[pltpu.SemaphoreType.DMA((8,))],
        )(
            jnp.stack([core, core * 2 + side]).astype(jnp.int32),
            expert_ids.T,
            gate_weights.T,
            tokens,
            w_in,
        )

        def norm(x, *others):
            return kernel_call(
                norm_body,
                shape(*x.shape),
                3,
                8 * x.size,
                4 * x.size,
            )(after(info, *others), x, norm_gain.reshape(1, model))

        def step(below, above, *beside):
            return both(up(below), down(above), *beside)[:2]

        first = across(raw)
        flops = 2 * rows * model * quarter
        nbytes = 2 * (rows * model + model * quarter)

        def near(*lefts):
            return kernel_call(
                functools.partial(near_body, depth, len(lefts)),
                (shape(rows, quarter, kind=F32), shape(rows, depth)),
                1 + len(lefts),
                flops,
                nbytes,
                places_for(blocks),
                len(blocks),
                BIG,
            )(info, *lefts, *blocks)

        def mine(first, part, *before, others=()):
            last = first + len(part) > wide
            outs = shape(rows, half) if last else shape(rows, quarter, kind=F32)
            number = min(first + len(part), wide)
            lines = shape(rows, wide, kind=F32) if last else shape(number, rows, kind=F32)
            return kernel_call(
                functools.partial(mine_body, depth, wide, first),
                (outs, lines),
                2 + len(part) + len(before),
                flops * len(part) // wide,
                nbytes * len(part) // wide,
            )(after(info, *others), normed, *part, *before)

        blocks = [block]
        below = above = block
        lat_mine = []
        for d in range(1, far):
            beside = []
            if d == 1:
                normed = norm(tokens, block)
                beside = [normed]
            else:
                begin = 0 if d == 2 else 2 * d - 3
                lat_mine = mine(begin, blocks[begin:], *lat_mine[::-1])
                beside = [*lat_mine]
            if d == 2:
                kept = lax.dynamic_slice_in_dim(
                    after(tokens, below), core * columns, columns, 1
                )
                beside += [kept, *pack(below)]
            elif d == 3:
                first = norm(first, below)
                beside += [first]
            below, above = step(below, above, *beside)
            blocks += [below, above]
        second = swap(after(first, below))
        near_there = near(first, second)
        begin = len(blocks) - 2
        lat_mine = mine(begin, blocks[begin:], *lat_mine[::-1])
        ends = step(below[: depth // 2], above[depth // 2 :], *near_there, *lat_mine)

        lat_there = kernel_call(
            functools.partial(far_body, depth),
            shape(rows, quarter),
            5,
            flops // wide,
            nbytes // wide,
        )(info, *near_there, *ends)
        lat_other = across(lat_there)
        out_step(lat_there)
        latent, gates = mine(len(blocks), ends, lat_other, *lat_mine[::-1])
        side_info = info.at[1].set(side.astype(jnp.int32))
        up_weight, down_weight = w_up[0].T, w_down[0]
        hidden = up_weight.shape[0]

        def expert(xs, columns, *others, swapped=None):
            size = sum(x.shape[0] for x in xs)
            out = shape(size, half)
            ys = swapped or [swap(x) for x in xs]
            return kernel_call(
                functools.partial(expert_body, columns),
                (out, out),
                4 + 2 * len(xs),
                4 * size * width * hidden,
                4 * hidden * width + 4 * size * width,
                [pltpu.VMEM((size, width), BF16), pltpu.VMEM((size, hidden), BF16)],
            )(after(info, *others), *xs, *ys, gates, up_weight, down_weight)

        def total(stay, given, more=None):
            t = stay.astype(F32) + given.astype(F32)
            return t if more is None else t + more.astype(F32)

        done = {}
        pairs = [(latent, latent)]
        for d in range(1, far + 1):
            below, above = pairs[-1]
            beside = []
            if d == 1:
                swapped = swap(latent)
                beside = [*out_blocks, swapped]
                hand(latent)
            elif d == 2:
                beside = [*pack(below), *handed]
                hand()
            elif d == 3:
                done[1] = expert(pairs[1], [(1, 0), (2, 0)], below)
                beside = [*done[1], *handed]
            if d == far:
                done[d - 1] = expert(pairs[d - 1], [(2 * d - 3, 0), (2 * d - 2, 0)])
                beside = [*done[d - 1]]
                below, above = below[:half_rows], above[half_rows:]
            pairs.append(step(below, above, *beside))
        below, above = pairs[far]
        done[far] = expert([below, above], [(wide - 1, 0), (wide - 1, half_rows)])

        given = swap(done[far][1])
        back = total(done[far][0], given).astype(BF16)
        out_step(*pairs[far])
        back = after(back, *out_blocks)
        done[far - 2] = expert(
            pairs[far - 2], [(2 * far - 5, 0), (2 * far - 4, 0)], back
        )
        beside = [*done[far - 2]]
        out_step(back)
        to_above, to_below = step(
            back[:half_rows], back[half_rows:], *beside, *out_blocks
        )
        for d in range(far - 1, 0, -1):
            given = swap(done[d][1])
            below = total(done[d][0][:rows], given[:rows])
            above = total(done[d][0][rows:], given[rows:])
            if d == far - 1:
                above = jnp.concatenate(
                    [above[:half_rows] + to_above.astype(F32), above[half_rows:]], axis=0
                )
                below = jnp.concatenate(
                    [below[:half_rows], below[half_rows:] + to_below.astype(F32)], axis=0
                )
            else:
                above, below = above + to_above.astype(F32), below + to_below.astype(F32)
            above, below = above.astype(BF16), below.astype(BF16)
            beside = []
            if d > 1 and d - 1 not in done:
                done[d - 1] = expert(
                    pairs[d - 1], [(2 * d - 3, 0), (2 * d - 2, 0)], to_above, to_below
                )
                beside += done[d - 1]
            if d == 2:
                done[0] = expert(
                    [latent], [(0, 0)], to_above, to_below, swapped=[swapped]
                )
                beside += done[0]
            if d == 1:
                given0 = swap(done[0][1])
                beside += [given0]
            if len(out_blocks) < 2 * far:
                out_step(to_above, to_below)
                beside += out_blocks
            while len(packs) < len(out_blocks) // 2:
                beside += pack(to_above)
            beside += handed[2:]
            if len(handed) < far:
                hand(to_above)
            if d == 1:
                full = kernel_call(
                    functools.partial(assemble_body, out_depth),
                    shape(width, columns),
                    1,
                    width * columns,
                    4 * width * columns,
                    [pltpu.SemaphoreType.DMA((1 + 2 * len(out_blocks),))],
                    1 + len(out_blocks) + len(handed),
                )(side_info, w_out, *out_blocks, *handed)
                beside = [*beside[: -len(handed)], full]
            to_above, to_below = step(above, below, *beside)
        mixture = total(done[0][0], given0, to_above)
        mixture = (mixture + to_below.astype(F32)).astype(BF16)
        partial = kernel_call(
            half_body,
            shape(rows, columns, kind=F32),
            4,
            rows * width * columns,
            width * columns + 6 * rows * columns,
        )(info, kept, mixture, full)
        back, partial = both(swap(mixture), partial)
        return pl.pallas_call(
            final_body,
            out_shape=shape(rows, columns),
            in_specs=[SMEM] + [VMEM] * 3,
            out_specs=ANY,
            scratch_shapes=[
                pltpu.VMEM((rows, columns), BF16),
                pltpu.SemaphoreType.DMA((columns // 512,)),
            ],
            compiler_params=pltpu.CompilerParams(vmem_limit_bytes=LIMIT),
        )(info, partial, back, full)

    return local


def solution(mesh):
    in_specs = (
        P(("groups", "wide"), None),
        P(),
        P("wide", None),
        P("wide", "narrow"),
        P("wide", None, "narrow"),
        P("wide", "narrow", None),
        P(("groups", "wide"), None),
        P(("groups", "wide"), None),
    )
    out_specs = P(("groups", "wide"), "narrow")
    local = make_local(ring_order(mesh))
    return jax.shard_map(
        local, mesh=mesh, in_specs=in_specs, out_specs=out_specs, check_vma=False
    )
```
